32 devices in a mesh: seq: 16 (over z, y, x), head: 2 (over core).
Axes of the slice: x: 2, y: 2, z: 4, core: 2. Of those that a mesh axis runs over, the one named last changes fastest.
Arguments:
- hidden_in: bfloat16 [4096, 4096], P('seq', 'head'), may hold values from -6 to 6
- proj_weight: bfloat16 [4096, 256], replicated, may hold values from -0.09375 to 0.09375
- head_input: bfloat16 [4096, 8192], P('seq', 'head'), may hold values from -6 to 6
- gate_input: bfloat16 [4096, 8192], P('seq', 'head'), may hold values from -11 to 11
- step_size: float32 [4096, 128], P('seq', 'head'), may hold values from 0 to 4, as said below
- decay_rate: float32 [128], P('head'), may hold values from 0 to 1, as said below
- norm_gain: float32 [8192], P('head'), may hold values from 0.1 to 1.9
Outputs:
- layer_out: bfloat16 [4096, 8192], P('seq', 'head')
The draws below stay inside these ranges and needn't reach their ends.
Inputs may be any that keep to these rules, and one draw needn't show every extreme that they name: `decay_rate`: positive. `step_size`: positive.
All inputs are finite; a program needn't handle non-finite values.
Results may differ from the reference program's by a relative error of at most 0.013.
Values may be sent and summed in bfloat16 or wider, within the bound.
No kernel may reach another device: no remote copies, remote signals or barrier semaphores. Data moves between devices by JAX's collectives and lax.ppermute only.
A program may use at most 128 MiB of HBM per device.

```python
import math
import jax
import jax.numpy as jnp
from jax import lax

D = 4096
HEADS = 128
HEAD_DIM = 64
STATE = 128
GROUP = 256
TOK_DEV = 256
TOKENS = 4096


def slow_heads(key):
    picked = jax.random.uniform(jax.random.fold_in(key, 101), (HEADS,))
    share = 0.5
    return picked < share


def slow_scale():
    return math.sqrt(32.0 / TOKENS)


def draw_step_size(key, part):
    slow = slow_heads(key)
    head_scale = jnp.where(slow, slow_scale(), 1.0)
    blocks = TOKENS // TOK_DEV
    spread = jnp.where(slow, math.log(4.0), math.log(2.0))
    level = jax.random.uniform(jax.random.fold_in(key, 202), (blocks, HEADS), minval=-1.0, maxval=1.0)
    factor = jnp.exp(level * spread[None, :])
    factor = jnp.repeat(factor, TOK_DEV, axis=0)
    jitter = jax.random.uniform(jax.random.fold_in(key, 303), (TOKENS, HEADS), minval=0.6, maxval=1.4)
    return (head_scale[None, :] * factor * jitter).astype(jnp.float32)


def draw_decay_rate(key, part):
    slow = slow_heads(key)
    slow_rate = jnp.exp(jax.random.uniform(jax.random.fold_in(key, 404), (HEADS,), minval=math.log(0.3), maxval=math.log(1.2))) / (TOKENS * slow_scale())
    fast_rate = jnp.exp(jax.random.uniform(jax.random.fold_in(key, 505), (HEADS,), minval=math.log(1.0 / 250.0), maxval=math.log(1.0 / 30.0)))
    return jnp.where(slow, slow_rate, fast_rate).astype(jnp.float32)


def draw_gate_input(key, part):
    columns = HEADS * HEAD_DIM
    ramp = jnp.arange(columns, dtype=jnp.float32) / (columns - 1)
    values = jnp.clip(jax.random.normal(jax.random.fold_in(key, 606), (TOKENS, columns), jnp.float32), -5.0, 5.0)
    values = values * (0.6 + 1.2 * ramp)[None, :]
    return values.astype(jnp.bfloat16)


def block_levels(rng, dims, cuts, least, high):
    def one(axis_at, shards_of):
        heights = jax.random.uniform(jax.random.fold_in(jax.random.fold_in(rng, 6), axis_at), (shards_of,), jnp.float32, least / len(cuts), high / len(cuts))
        return jnp.repeat(jnp.exp(heights), dims[axis_at] // shards_of).reshape((-1,) + (1,) * (len(dims) - axis_at - 1))

    factor_of = one(*cuts[0])
    for cut in cuts[1:]:
        factor_of = factor_of * one(*cut)
    return factor_of


def bell_draw(own_key, extent, scale, bound, shards=(), kind=jnp.bfloat16):
    values = jax.random.normal(own_key, extent, jnp.float32) * scale
    if len(shards) > 0:
        values = block_levels(own_key, extent, shards, -0.22, 0.18) * values
    return jnp.clip(values, min=-bound, max=bound).astype(kind)


def setup_inputs(seed: int = 0) -> dict:
    key_list = jax.random.split(jax.random.key(seed), 8)
    return {
        "hidden_in": bell_draw(key_list[0], (TOKENS, D), 1.0, 6.0, ((0, 16), (1, 2))),
        "proj_weight": bell_draw(key_list[1], (D, 2 * STATE), D ** -0.5, 0.09375),
        "head_input": bell_draw(key_list[2], (TOKENS, HEADS * HEAD_DIM), 1.0, 6.0, ((0, 16), (1, 2))),
        "gate_input": draw_gate_input(jax.random.fold_in(key_list[7], 71), 0),
        "step_size": draw_step_size(jax.random.fold_in(key_list[7], 71), 0),
        "decay_rate": draw_decay_rate(jax.random.fold_in(key_list[7], 71), 0),
        "norm_gain": jnp.clip(1.0 + 0.18 * jax.random.normal(key_list[6], (HEADS * HEAD_DIM,), jnp.float32), 0.1, 1.9),
    }


def reference(hidden_in, proj_weight, head_input, gate_input, step_size, decay_rate, norm_gain):
    projected = jnp.dot(hidden_in, proj_weight, preferred_element_type=jnp.float32).astype(jnp.bfloat16)
    count = TOKENS // GROUP
    b_rows = projected[:, :STATE].reshape(count, GROUP, STATE)
    c_rows = projected[:, STATE:].reshape(count, GROUP, STATE)
    log_decay = -step_size * decay_rate[None, :]
    cumulative = jnp.cumsum(log_decay.reshape(count, GROUP, HEADS), axis=1)
    scaled = (head_input.reshape(TOKENS, HEADS, HEAD_DIM).astype(jnp.float32) * step_size[:, :, None]).astype(jnp.bfloat16)
    scaled = scaled.reshape(count, GROUP, HEADS, HEAD_DIM)
    positions = jnp.arange(GROUP, dtype=jnp.int32)
    causal = positions[:, None] >= positions[None, :]

    def one_group(carried, pieces):
        b_here, c_here, cum_here, x_here = pieces
        scores = jnp.dot(c_here, b_here.T, preferred_element_type=jnp.float32)
        cum_heads = cum_here.T
        gap = cum_heads[:, :, None] - cum_heads[:, None, :]
        weights = jnp.exp(jnp.where(causal[None], gap, -jnp.inf))
        mixing = lax.optimization_barrier((scores[None] * weights).astype(jnp.bfloat16))
        inner = jnp.einsum('hts,shp->thp', mixing.astype(jnp.float32), x_here.astype(jnp.float32))
        carried_low = lax.optimization_barrier(carried.astype(jnp.bfloat16))
        outer = jnp.einsum('tn,hpn->thp', c_here.astype(jnp.float32), carried_low.astype(jnp.float32))
        outer = outer * jnp.exp(cum_here)[:, :, None]
        tail = jnp.exp(cum_here[-1][None, :] - cum_here)
        weighted = lax.optimization_barrier((tail[:, :, None] * x_here.astype(jnp.float32)).astype(jnp.bfloat16))
        fresh = jnp.einsum('shp,sn->hpn', weighted.astype(jnp.float32), b_here.astype(jnp.float32))
        updated = jnp.exp(cum_here[-1])[:, None, None] * carried + fresh
        return (updated, inner + outer)
    start = jnp.zeros((HEADS, HEAD_DIM, STATE), jnp.float32)
    final, outputs = lax.scan(one_group, start, (b_rows, c_rows, cumulative, scaled))
    mixed = outputs.reshape(TOKENS, HEADS * HEAD_DIM)
    gated = mixed * jax.nn.silu(gate_input.astype(jnp.float32))
    mean_square = lax.optimization_barrier(jnp.mean(gated * gated, axis=1, keepdims=True))
    return (gated * lax.rsqrt(mean_square + 1e-05) * norm_gain[None, :]).astype(jnp.bfloat16)
```

```python
import functools

import jax
import jax.numpy as jnp
from jax import lax
from jax.experimental import pallas as pl
from jax.experimental.pallas import tpu as pltpu
from jax.sharding import PartitionSpec as P

HEAD_DIM = 64
STATE = 128
GROUP = 256
EPS = 1e-05
EXTRA = 16
LIMIT = 48 * 1024 * 1024

F32 = jnp.float32
BF16 = jnp.bfloat16


def params():
    return pltpu.CompilerParams(vmem_limit_bytes=LIMIT)


def cost(flops, moved, exps=0):
    return pl.CostEstimate(flops=flops, bytes_accessed=moved, transcendentals=exps)


def halves(value, count):
    terms = []
    for _ in range(count):
        term = value.astype(BF16)
        terms.append(term)
        value = value - term.astype(F32)
    return jnp.concatenate(terms, axis=1)


def spread(value, first_head, heads, lanes, width, count):
    row = lax.broadcasted_iota(jnp.int32, (heads, lanes), 0)
    col = lax.broadcasted_iota(jnp.int32, (heads, lanes), 1)
    pick = jnp.where(row == first_head + col // width, 1.0, 0.0).astype(BF16)
    pick = jnp.concatenate([pick] * count, axis=0)
    return jnp.dot(halves(value, count), pick, preferred_element_type=F32)


def project_kernel(which, hidden, weight, out):
    @pl.when(pl.program_id(0) == 0)
    def _():
        out[...] = jnp.zeros_like(out)

    out[...] += jnp.dot(hidden[...], weight[...], preferred_element_type=F32)


def project(which, hidden, weight):
    rows, depth = hidden.shape
    cols = weight.shape[1]
    tiles = 4
    tile = depth // tiles
    return pl.pallas_call(
        project_kernel,
        grid_spec=pltpu.PrefetchScalarGridSpec(
            num_scalar_prefetch=1,
            grid=(tiles,),
            in_specs=[
                pl.BlockSpec((rows, tile), lambda k, w: (0, k)),
                pl.BlockSpec((tile, cols), lambda k, w: (w[0] * tiles + k, 0)),
            ],
            out_specs=pl.BlockSpec((rows, cols), lambda k, w: (0, 0)),
        ),
        out_shape=jax.ShapeDtypeStruct((rows, cols), F32),
        compiler_params=params(),
        cost_estimate=cost(2 * rows * depth * cols, 2 * rows * depth + 2 * depth * cols),
        name="project",
    )(which, hidden, weight)


def decay_kernel(step, rate, x, weighted, cum, cum_rows, ends, held):
    rows, heads = step.shape
    lanes = x.shape[1]
    at = pl.program_id(0)

    @pl.when(at == 0)
    def _():
        log_decay = -step[...] * rate[...]
        t = lax.broadcasted_iota(jnp.int32, (rows, rows), 0)
        s = lax.broadcasted_iota(jnp.int32, (rows, rows), 1)
        lower = jnp.where(s <= t, 1.0, 0.0).astype(BF16)
        parts = jnp.dot(lower, halves(log_decay, 3), preferred_element_type=F32)
        total = parts[:, :heads] + (parts[:, heads : 2 * heads] + parts[:, 2 * heads :])
        cum[...] = total
        cum_rows[...] = total.T
        held[:rows, :] = jnp.exp(total[rows - 1 :, :] - total) * step[...]
        held[rows:, :] = jnp.broadcast_to(jnp.exp(total[rows - 1 :, :]), (16, heads))

    wide = spread(held[...], at * (lanes // HEAD_DIM), heads, lanes, HEAD_DIM, 3)
    weighted[...] = (x[...].astype(F32) * wide[:rows]).astype(BF16)
    last = wide[rows:]
    high = last.astype(BF16).astype(F32)
    middle = (last - high).astype(BF16).astype(F32)
    low = last - high - middle
    row = lax.broadcasted_iota(jnp.int32, last.shape, 0)
    ends[...] = jnp.where(row == 0, high, jnp.where(row == 1, middle, low)).astype(BF16)


def decays(step, rate, x):
    rows, heads = step.shape
    cols = x.shape[1]
    tiles = min(4, cols // STATE)
    tile = cols // tiles
    whole = lambda i: (0, 0)
    return pl.pallas_call(
        decay_kernel,
        grid=(tiles,),
        in_specs=[
            pl.BlockSpec((rows, heads), whole),
            pl.BlockSpec((1, heads), whole),
            pl.BlockSpec((rows, tile), lambda i: (0, i)),
        ],
        out_specs=[
            pl.BlockSpec((rows, tile), lambda i: (0, i)),
            pl.BlockSpec((rows, heads), whole),
            pl.BlockSpec((heads, rows), whole),
            pl.BlockSpec((16, tile), lambda i: (0, i)),
        ],
        out_shape=[
            jax.ShapeDtypeStruct((rows, cols), BF16),
            jax.ShapeDtypeStruct((rows, heads), F32),
            jax.ShapeDtypeStruct((heads, rows), F32),
            jax.ShapeDtypeStruct((16, cols), BF16),
        ],
        scratch_shapes=[pltpu.VMEM((rows + 16, heads), F32)],
        compiler_params=params(),
        cost_estimate=cost(2 * rows * cols * 256, 4 * rows * cols, 2 * rows * heads),
        name="decays",
    )(step, rate, x)


def fresh_kernel(place, size, parts, weighted, ends, proj, *slices):
    total = parts[0][...]
    for part in parts[1:]:
        total = total + part[...]
    rounded = total.astype(BF16)
    proj[...] = rounded
    width = weighted.shape[1] // size
    b_rows = rounded[:, :STATE]
    for m in range(size):
        owner = place[0] ^ m
        cols = pl.ds(pl.multiple_of(owner * width, width), width)
        state = lax.dot_general(
            b_rows, weighted[:, cols], (((0,), (0,)), ((), ())), preferred_element_type=F32
        )
        slices[m][:STATE, :] = state.astype(BF16)
        slices[m][STATE:, :] = ends[:, cols]


def fresh_states(place, size, parts, weighted, ends):
    rows, cols = weighted.shape
    width = cols // size
    n = len(parts)

    def body(place, *refs):
        fresh_kernel(place, size, refs[:n], *refs[n:])

    return pl.pallas_call(
        body,
        in_specs=[pl.BlockSpec(memory_space=pltpu.SMEM)]
        + [pl.BlockSpec(memory_space=pltpu.VMEM)] * (n + 2),
        out_specs=[pl.BlockSpec(memory_space=pltpu.VMEM)] * (1 + size),
        out_shape=[jax.ShapeDtypeStruct((rows, 2 * STATE), BF16)]
        + [jax.ShapeDtypeStruct((STATE + EXTRA, width), BF16)] * size,
        compiler_params=params(),
        cost_estimate=cost(2 * rows * cols * STATE, 4 * rows * cols),
        name="fresh",
    )(place, *parts, weighted, ends)


def gather_order(place, size, slices, states, factors):
    for m in range(size):
        at = place[0] ^ m
        states[at] = slices[m][:STATE, :].astype(F32)
        tail = slices[m][STATE:, :].astype(F32)
        factors[at] = tail[:8, :]


def factor_of(factors, j):
    tail = factors[j]
    return tail[0:1] + (tail[1:2] + tail[2:3])


def total_kernel(size, place, *refs):
    slices, (out, decay, states, factors) = refs[:size], refs[size:]
    gather_order(place, size, slices, states, factors)
    running = states[0]
    product = factor_of(factors, 0)
    for j in range(1, size):
        step = factor_of(factors, j)
        running = running * step + states[j]
        product = product * step
    out[...] = running.astype(BF16)
    decay[...] = jnp.broadcast_to(product, decay.shape)


def group_total(place, slices):
    size = len(slices)
    width = slices[0].shape[1]
    return pl.pallas_call(
        functools.partial(total_kernel, size),
        in_specs=[pl.BlockSpec(memory_space=pltpu.SMEM)]
        + [pl.BlockSpec(memory_space=pltpu.VMEM)] * size,
        out_specs=[pl.BlockSpec(memory_space=pltpu.VMEM)] * 2,
        out_shape=[
            jax.ShapeDtypeStruct((STATE, width), BF16),
            jax.ShapeDtypeStruct((8, width), F32),
        ],
        scratch_shapes=[
            pltpu.VMEM((size, STATE, width), F32),
            pltpu.VMEM((size, 8, width), F32),
        ],
        compiler_params=params(),
        cost_estimate=cost(2 * size * STATE * width, 2 * size * STATE * width),
        name="total",
    )(place, *slices)


def enter_kernel(size, place, *refs):
    slices, before, outs = refs[:size], refs[size], refs[size + 1 : 2 * size + 1]
    states, factors = refs[2 * size + 1 :]
    gather_order(place, size, slices, states, factors)
    running = before[...].astype(F32)
    for j in range(size):
        following = running * factor_of(factors, j) + states[j]
        states[j] = running
        running = following
    for m in range(size):
        outs[m][...] = states[place[0] ^ m].astype(BF16)


def entering_states(place, slices, before):
    size = len(slices)
    width = slices[0].shape[1]
    return pl.pallas_call(
        functools.partial(enter_kernel, size),
        in_specs=[pl.BlockSpec(memory_space=pltpu.SMEM)]
        + [pl.BlockSpec(memory_space=pltpu.VMEM)] * (size + 1),
        out_specs=[pl.BlockSpec(memory_space=pltpu.VMEM)] * size,
        out_shape=[jax.ShapeDtypeStruct((STATE, width), BF16)] * size,
        scratch_shapes=[
            pltpu.VMEM((size, STATE, width), F32),
            pltpu.VMEM((size, 8, width), F32),
        ],
        compiler_params=params(),
        cost_estimate=cost(2 * size * STATE * width, 4 * size * STATE * width),
        name="entering",
    )(place, *slices, before)


def inner_kernel(heads, proj, cum, cum_rows, step, x, gate, base, slope, scores, mixed):
    rows = cum.shape[0]
    lanes = x.shape[1]
    here = lanes // HEAD_DIM
    half = rows // 2
    at = pl.program_id(0)

    @pl.when(at == 0)
    def _():
        scores[...] = lax.dot_general(
            proj[:, STATE:], proj[:, :STATE], (((1,), (1,)), ((), ())), preferred_element_type=F32
        )

    first = at * here
    columns = spread(cum[...], first, heads, here * STATE, STATE, 3)
    scaled = (x[...].astype(F32) * spread(step[...], first, heads, lanes, HEAD_DIM, 3)).astype(BF16)
    t = lax.broadcasted_iota(jnp.int32, (half, half), 0)
    s = lax.broadcasted_iota(jnp.int32, (half, half), 1)
    causal = s <= t
    for k in range(here):
        col = columns[:, k * STATE : (k + 1) * STATE]
        row = cum_rows[k : k + 1, :]
        blocks = []
        for i, j in ((0, 0), (1, 0), (1, 1)):
            gap = col[i * half : (i + 1) * half] - row[:, j * half : (j + 1) * half]
            if i == j:
                gap = jnp.where(causal, gap, -jnp.inf)
            piece = scores[i * half : (i + 1) * half, j * half : (j + 1) * half]
            blocks.append((piece * jnp.exp(gap)).astype(BF16))
        mine = scaled[:, k * HEAD_DIM : (k + 1) * HEAD_DIM]
        mixed[:half, k * HEAD_DIM : (k + 1) * HEAD_DIM] = jnp.dot(
            blocks[0], mine[:half], preferred_element_type=F32
        )
        mixed[half:, k * HEAD_DIM : (k + 1) * HEAD_DIM] = jnp.dot(
            jnp.concatenate(blocks[1:], axis=1), mine, preferred_element_type=F32
        )
    g = gate[...].astype(F32)
    silu = g / (1.0 + jnp.exp(-g))
    grown = spread(jnp.exp(cum[...]), first, heads, lanes, HEAD_DIM, 3)
    base[...] = mixed[...] * silu
    slope[...] = grown * silu


def inside(proj, cum, cum_rows, step, x, gate):
    rows, heads = step.shape
    cols = x.shape[1]
    here = min(8, heads)
    tile = here * HEAD_DIM
    whole = lambda i: (0, 0)
    part = lambda i: (0, i)
    return pl.pallas_call(
        functools.partial(inner_kernel, heads),
        grid=(heads // here,),
        in_specs=[
            pl.BlockSpec((rows, 2 * STATE), whole),
            pl.BlockSpec((rows, heads), whole),
            pl.BlockSpec((here, rows), lambda i: (i, 0)),
            pl.BlockSpec((rows, heads), whole),
            pl.BlockSpec((rows, tile), part),
            pl.BlockSpec((rows, tile), part),
        ],
        out_specs=[pl.BlockSpec((rows, tile), part)] * 2,
        out_shape=[jax.ShapeDtypeStruct((rows, cols), F32)] * 2,
        scratch_shapes=[pltpu.VMEM((rows, rows), F32), pltpu.VMEM((rows, tile), F32)],
        compiler_params=params(),
        cost_estimate=cost(8 * rows * rows * cols, 12 * rows * cols, rows * rows * heads),
        name="inner",
    )(proj, cum, cum_rows, step, x, gate)


def outer_kernel(size, place, proj, base, slope, *refs):
    states, (gated, squares) = refs[:size], refs[size:]
    c_rows = proj[:, STATE:]
    width = base.shape[1] // size
    total = jnp.zeros(squares.shape, F32)
    for m in range(size):
        cols = pl.ds(pl.multiple_of((place[0] ^ m) * width, width), width)
        read = jnp.dot(c_rows, states[m][...], preferred_element_type=F32)
        value = base[:, cols] + slope[:, cols] * read
        gated[:, cols] = value
        square = value * value
        for k in range(width // STATE):
            total = total + square[:, k * STATE : (k + 1) * STATE]
    squares[...] = total


def outer_part(place, proj, base, slope, states):
    size = len(states)
    rows, cols = base.shape
    return pl.pallas_call(
        functools.partial(outer_kernel, size),
        in_specs=[pl.BlockSpec(memory_space=pltpu.SMEM)]
        + [pl.BlockSpec(memory_space=pltpu.VMEM)] * (size + 3),
        out_specs=[pl.BlockSpec(memory_space=pltpu.VMEM)] * 2,
        out_shape=[
            jax.ShapeDtypeStruct((rows, cols), F32),
            jax.ShapeDtypeStruct((rows, STATE), F32),
        ],
        compiler_params=params(),
        cost_estimate=cost(2 * rows * cols * STATE, 12 * rows * cols),
        name="outer",
    )(place, proj, base, slope, *states)


def norm_kernel(count, n, *refs):
    parts, (gated, gain, out) = refs[:n], refs[n:]
    total = parts[0][...]
    for part in parts[1:]:
        total = total + part[...]
    mean = jnp.sum(total, axis=1, keepdims=True) * (1.0 / count)
    out[...] = (gated[...] * lax.rsqrt(mean + EPS) * gain[...]).astype(BF16)


def normalise(count, parts, gated, gain):
    rows, cols = gated.shape
    n = len(parts)
    tiles = 4
    tile = rows // tiles
    row = lambda i: (i, 0)
    return pl.pallas_call(
        functools.partial(norm_kernel, count, n),
        grid=(tiles,),
        in_specs=[pl.BlockSpec((tile, STATE), row)] * n
        + [pl.BlockSpec((tile, cols), row), pl.BlockSpec((1, cols), lambda i: (0, 0))],
        out_specs=pl.BlockSpec((tile, cols), row),
        out_shape=jax.ShapeDtypeStruct((rows, cols), BF16),
        compiler_params=params(),
        cost_estimate=cost(4 * rows * cols, 6 * rows * cols),
        name="norm",
    )(*parts, gated, gain)


def swap(value, axis, mask):
    pairs = [(i, i ^ mask) for i in range(lax.axis_size(axis))]
    return lax.ppermute(value, axis, pairs)


def terms_of_sum(value, axis):
    mask = 1
    terms = [value]
    while mask < lax.axis_size(axis):
        if len(terms) > 1:
            terms = [sum(terms[1:], terms[0])]
        terms.append(swap(terms[0], axis, mask))
        mask *= 2
    return terms


def shards(hidden, weight, head_input, gate_input, step, rate, gain):
    heads = step.shape[1]
    devices = lax.axis_size("seq")
    size = 8
    while devices % size or heads % size or (heads // size * HEAD_DIM) % STATE:
        size //= 2
    groups = devices // size
    place = (lax.axis_index("seq") % size).astype(jnp.int32).reshape(1)
    which = lax.axis_index("head").astype(jnp.int32).reshape(1)

    with jax.named_scope("projection"):
        parts = terms_of_sum(project(which, hidden, weight), "head")
    with jax.named_scope("decays"):
        weighted, cum, cum_rows, ends = decays(step, rate.reshape(1, heads), head_input)
    with jax.named_scope("states"):
        proj, *mine = fresh_states(place, size, parts, weighted, ends)
    with jax.named_scope("to_owners"):
        slices = [mine[0]] + [swap(mine[m], "seq", m) for m in range(1, size)]
    with jax.named_scope("groups"):
        total, decay = group_total(place, slices)
        up = [(i, i + size) for i in range(devices - size)]
        before = jnp.zeros_like(total)
        for k in range(groups - 1):
            if k > 0:
                sent = (before.astype(F32) * decay[:1] + total.astype(F32)).astype(BF16)
            else:
                sent = total
            before = lax.ppermute(sent, "seq", up)
    with jax.named_scope("inner"):
        base, slope = inside(proj, cum, cum_rows, step, head_input, gate_input)
    with jax.named_scope("from_owners"):
        outs = entering_states(place, slices, before)
        states = [outs[0]] + [swap(outs[m], "seq", m) for m in range(1, size)]
    with jax.named_scope("outer"):
        gated, squares = outer_part(place, proj, base, slope, states)
    with jax.named_scope("norm"):
        count = head_input.shape[1] * lax.axis_size("head")
        sums = terms_of_sum(squares, "head")
        return normalise(count, sums, gated, gain.reshape(1, -1))


def solution(mesh):
    in_specs = (
        P("seq", "head"),
        P(),
        P("seq", "head"),
        P("seq", "head"),
        P("seq", "head"),
        P("head"),
        P("head"),
    )
    return jax.shard_map(
        shards, mesh=mesh, in_specs=in_specs, out_specs=P("seq", "head"), check_vma=False
    )
```

```python
import functools

import jax
import jax.numpy as jnp
from jax import lax
from jax.experimental import pallas as pl
from jax.experimental.pallas import tpu as pltpu
from jax.sharding import PartitionSpec as P

HEAD_DIM = 64
STATE = 128
GROUP = 256
EPS = 1e-05
EXTRA = 16
LIMIT = 16 * 1024 * 1024
WIDE = 62 * 1024 * 1024
LOG2E = 1.4426950408889634

F32 = jnp.float32
BF16 = jnp.bfloat16
VMEM = pl.BlockSpec(memory_space=pltpu.VMEM)
SMEM = pl.BlockSpec(memory_space=pltpu.SMEM)


def params(limit=LIMIT):
    return pltpu.CompilerParams(vmem_limit_bytes=limit)


def cost(flops, moved, exps=0):
    return pl.CostEstimate(flops=flops, bytes_accessed=moved, transcendentals=exps)


def position(size):
    return lax.axis_index("seq") % size


def halves(value, count):
    terms = []
    for _ in range(count):
        term = value.astype(BF16)
        terms.append(term)
        value = value - term.astype(F32)
    return jnp.concatenate(terms, axis=1)


def picks(first_head, heads, lanes, width, count):
    row = lax.broadcasted_iota(jnp.int32, (heads, lanes), 0)
    col = lax.broadcasted_iota(jnp.int32, (heads, lanes), 1)
    pick = jnp.where(row == first_head + col // width, 1.0, 0.0).astype(BF16)
    return jnp.concatenate([pick] * count, axis=0)


def project_kernel(tiles, hidden, weight, out, rows_held, weight_held, sems):
    tile = hidden.shape[1] // tiles
    copies = []
    for k in range(tiles):
        row = pl.multiple_of(lax.axis_index("head") * hidden.shape[1] + k * tile, tile)
        pair = (
            pltpu.make_async_copy(
                hidden.at[:, pl.ds(k * tile, tile)], rows_held.at[k], sems.at[0, k]
            ),
            pltpu.make_async_copy(weight.at[pl.ds(row, tile), :], weight_held.at[k], sems.at[1, k]),
        )
        for copy in pair:
            copy.start()
        copies.append(pair)
    total = jnp.zeros(out.shape, F32)
    for k in range(tiles):
        for copy in copies[k]:
            copy.wait()
        total = total + jnp.dot(rows_held[k], weight_held[k], preferred_element_type=F32)
    out[...] = total


def project(hidden, weight):
    rows, depth = hidden.shape
    cols = weight.shape[1]
    tiles = 4
    tile = depth // tiles
    return pl.pallas_call(
        functools.partial(project_kernel, tiles),
        in_specs=[
            pl.BlockSpec(memory_space=pltpu.HBM),
            pl.BlockSpec(memory_space=pltpu.HBM),
        ],
        out_specs=VMEM,
        out_shape=jax.ShapeDtypeStruct((rows, cols), F32),
        scratch_shapes=[
            pltpu.VMEM((tiles, rows, tile), BF16),
            pltpu.VMEM((tiles, tile, cols), BF16),
            pltpu.SemaphoreType.DMA((2, tiles)),
        ],
        compiler_params=params(WIDE),
        cost_estimate=cost(2 * rows * depth * cols, 2 * rows * depth + 2 * depth * cols),
        name="project",
    )(hidden, weight)


def decay_kernel(step_rows, rate, x, weighted, cum, cum_rows, ends, step_out):
    heads, rows = step_rows.shape
    cols = x.shape[1]
    step = step_rows[...].T
    step_out[...] = step
    log_decay = -step * rate[...]
    t = lax.broadcasted_iota(jnp.int32, (rows, rows), 0)
    s = lax.broadcasted_iota(jnp.int32, (rows, rows), 1)
    lower = jnp.where(s <= t, 1.0, 0.0).astype(BF16)
    parts = jnp.dot(lower, halves(log_decay, 3), preferred_element_type=F32)
    total = parts[:, :heads] + (parts[:, heads : 2 * heads] + parts[:, 2 * heads :])
    cum[...] = total
    cum_rows[...] = total.T
    last = total[rows - 1 :, :]
    factor = halves(jnp.exp(last - total) * step, 3)
    final = halves(jnp.broadcast_to(jnp.exp(last), (EXTRA, heads)), 3)
    both = jnp.concatenate([factor, final], axis=0)
    lanes = min(1024, cols)
    for at in range(cols // lanes):
        here = slice(at * lanes, (at + 1) * lanes)
        pick = picks(at * (lanes // HEAD_DIM), heads, lanes, HEAD_DIM, 3)
        wide = jnp.dot(both, pick, preferred_element_type=F32)
        weighted[:, here] = (x[:, here].astype(F32) * wide[:rows]).astype(BF16)
        end = wide[rows:]
        high = end.astype(BF16).astype(F32)
        middle = (end - high).astype(BF16).astype(F32)
        low = end - high - middle
        row = lax.broadcasted_iota(jnp.int32, end.shape, 0)
        ends[:, here] = jnp.where(row == 0, high, jnp.where(row == 1, middle, low)).astype(BF16)


def decays(step_rows, rate, x):
    heads, rows = step_rows.shape
    cols = x.shape[1]
    return pl.pallas_call(
        decay_kernel,
        in_specs=[VMEM] * 3,
        out_specs=[VMEM] * 5,
        out_shape=[
            jax.ShapeDtypeStruct((rows, cols), BF16),
            jax.ShapeDtypeStruct((rows, heads), F32),
            jax.ShapeDtypeStruct((heads, rows), F32),
            jax.ShapeDtypeStruct((EXTRA, cols), BF16),
            jax.ShapeDtypeStruct((rows, heads), F32),
        ],
        compiler_params=params(),
        cost_estimate=cost(2 * rows * cols * 256, 4 * rows * cols, 2 * rows * heads),
        name="decays",
    )(step_rows, rate, x)


def fresh_kernel(n, *refs):
    parts, (weighted, ends, proj), slices = refs[:n], refs[n : n + 3], refs[n + 3 :]
    size = len(slices)
    place = position(size)
    total = parts[0][...]
    for part in parts[1:]:
        total = total + part[...]
    rounded = total.astype(BF16)
    proj[...] = rounded
    width = weighted.shape[1] // size
    b_rows = rounded[:, :STATE]
    for m in range(size):
        cols = pl.ds(pl.multiple_of((place ^ m) * width, width), width)
        state = lax.dot_general(
            b_rows, weighted[:, cols], (((0,), (0,)), ((), ())), preferred_element_type=F32
        )
        slices[m][:STATE, :] = state.astype(BF16)
        slices[m][STATE:, :] = ends[:, cols]


def fresh_states(size, parts, weighted, ends):
    rows, cols = weighted.shape
    width = cols // size
    n = len(parts)
    return pl.pallas_call(
        functools.partial(fresh_kernel, n),
        in_specs=[VMEM] * (n + 2),
        out_specs=[VMEM] * (1 + size),
        out_shape=[jax.ShapeDtypeStruct((rows, 2 * STATE), BF16)]
        + [jax.ShapeDtypeStruct((STATE + EXTRA, width), BF16)] * size,
        compiler_params=params(),
        cost_estimate=cost(2 * rows * cols * STATE, 4 * rows * cols),
        name="fresh",
    )(*parts, weighted, ends)


def gather_factors(order, slices, factors):
    place = position(len(order))
    for m, piece in zip(order, slices):
        tail = piece[STATE:, :].astype(F32)
        factors[place ^ m] = jnp.broadcast_to(tail[0:1] + (tail[1:2] + tail[2:3]), factors.shape[1:])


def total_kernel(order, *refs):
    place = position(len(order))
    slices, (out, decay, factors) = refs[:-3], refs[-3:]
    size = len(slices)
    gather_factors(order, slices, factors)
    product = jnp.ones(factors.shape[1:], F32)
    for j in reversed(range(size)):
        factor = factors[j]
        factors[j] = product
        product = product * factor
    decay[...] = product
    total = jnp.zeros(out.shape, F32)
    for m, piece in zip(order, slices):
        total = total + factors[place ^ m][:1] * piece[:STATE, :].astype(F32)
    out[...] = total.astype(BF16)


def group_total(order, slices):
    size = len(slices)
    width = slices[0].shape[1]
    return pl.pallas_call(
        functools.partial(total_kernel, order),
        in_specs=[VMEM] * size,
        out_specs=[VMEM] * 2,
        out_shape=[
            jax.ShapeDtypeStruct((STATE, width), BF16),
            jax.ShapeDtypeStruct((8, width), F32),
        ],
        scratch_shapes=[pltpu.VMEM((size, 8, width), F32)],
        compiler_params=params(),
        cost_estimate=cost(2 * size * STATE * width, 2 * size * STATE * width),
        name="total",
    )(*slices)


def local_kernel(order, *refs):
    place = position(len(order))
    slices, (states, scales, ordered, factors) = refs[:-4], refs[-4:]
    size = len(slices)
    gather_factors(order, slices, factors)
    for m, piece in zip(order, slices):
        ordered[place ^ m] = piece[:STATE, :]
    running = jnp.zeros(states.shape[1:], F32)
    product = jnp.ones(factors.shape[1:], F32)
    for j in range(size):
        at = jnp.int32(0)
        for i, m in enumerate(order):
            at = jnp.where(place ^ j == m, i, at)
        states[at] = running
        scales[at] = product
        running = running * factors[j][:1] + ordered[j].astype(F32)
        product = product * factors[j]


def local_states(order, slices):
    size = len(slices)
    width = slices[0].shape[1]
    return pl.pallas_call(
        functools.partial(local_kernel, order),
        in_specs=[VMEM] * size,
        out_specs=[VMEM] * 2,
        out_shape=[
            jax.ShapeDtypeStruct((size, STATE, width), F32),
            jax.ShapeDtypeStruct((size, 8, width), F32),
        ],
        scratch_shapes=[
            pltpu.VMEM((size, STATE, width), BF16),
            pltpu.VMEM((size, 8, width), F32),
        ],
        compiler_params=params(),
        cost_estimate=cost(2 * size * STATE * width, 6 * size * STATE * width),
        name="local",
    )(*slices)


def enter_kernel(states, scales, before, token, *outs):
    group = lax.axis_index("seq") // len(outs)
    entering = jnp.where(group > 0, before[...].astype(F32), 0.0)
    for m, out in enumerate(outs):
        out[...] = (entering * scales[m][:1] + states[m]).astype(BF16)


def entering_states(states, scales, before, token):
    size, _, width = states.shape
    return pl.pallas_call(
        enter_kernel,
        in_specs=[VMEM] * 4,
        out_specs=[VMEM] * size,
        out_shape=[jax.ShapeDtypeStruct((STATE, width), BF16)] * size,
        compiler_params=params(),
        cost_estimate=cost(2 * size * STATE * width, 6 * size * STATE * width),
        name="entering",
    )(states, scales, before, token)


def inner_kernel(order, proj, cum, cum_rows, step, x, gate, base, slope, token, scores, mixed):
    rows, heads = cum.shape
    width = base.shape[2]
    here = width // HEAD_DIM
    half = rows // 2
    place = position(len(order))
    all_scores = lax.dot_general(
        proj[:, STATE:], proj[:, :STATE], (((1,), (1,)), ((), ())), preferred_element_type=F32
    )
    t = lax.broadcasted_iota(jnp.int32, (half, half), 0)
    s = lax.broadcasted_iota(jnp.int32, (half, half), 1)
    scores[0] = jnp.where(s <= t, all_scores[:half, :half], 0.0)
    scores[1] = jnp.where(s <= t, all_scores[half:, half:], 0.0)
    lower = all_scores[half:, :half].astype(BF16)
    total = cum[...]
    middle = total[half - 1 : half, :]
    grown = jnp.exp(total)
    later = jnp.concatenate(
        [jnp.exp(middle - total[:half]) * step[:half, :], jnp.exp(total[half:] - middle)], axis=0
    )
    per_head = jnp.concatenate([halves(value, 3) for value in (step[...], grown, later)], axis=0)
    parts = halves(total * LOG2E, 3)
    token[...] = jnp.zeros(token.shape, F32)

    def one(at, carry):
        owner = place ^ entry(order, at)
        cols = pl.ds(pl.multiple_of(owner * width, width), width)
        first = owner * here
        wide = jnp.dot(per_head, picks(first, heads, width, HEAD_DIM, 3), preferred_element_type=F32)
        columns = jnp.dot(
            parts, picks(first, heads, here * half, half, 3), preferred_element_type=F32
        )
        values = x[:, cols].astype(F32)
        scaled = (values * wide[:rows]).astype(BF16)
        early = (values[:half] * wide[2 * rows : 2 * rows + half]).astype(BF16)
        cross = jnp.dot(lower, early, preferred_element_type=F32) * wide[2 * rows + half :]
        for k in range(here):
            line = cum_rows[pl.ds(first + k, 1), :] * LOG2E
            mine = slice(k * HEAD_DIM, (k + 1) * HEAD_DIM)
            for i in range(2):
                span = slice(i * half, (i + 1) * half)
                gap = columns[span, k * half : (k + 1) * half] - line[:, span]
                block = (scores[i] * jnp.exp2(jnp.minimum(gap, 0.0))).astype(BF16)
                mixed[span, mine] = jnp.dot(block, scaled[span, mine], preferred_element_type=F32)
        g = gate[:, cols].astype(F32)
        silu = g / (1.0 + jnp.exp(-g))
        base[at, :half, :] = mixed[:half, :] * silu[:half]
        base[at, half:, :] = (mixed[half:, :] + cross) * silu[half:]
        slope[at] = wide[rows : 2 * rows] * silu
        return carry

    lax.fori_loop(0, base.shape[0], one, 0)


def entry(order, at):
    value = jnp.int32(order[0])
    for i, m in enumerate(order):
        value = jnp.where(at == i, m, value)
    return value


def inside(order, proj, cum, cum_rows, step, x, gate):
    rows, heads = step.shape
    n = len(order)
    width = x.shape[1] // n
    return pl.pallas_call(
        functools.partial(inner_kernel, order),
        in_specs=[VMEM] * 6,
        out_specs=[VMEM] * 3,
        out_shape=[jax.ShapeDtypeStruct((n, rows, width), F32)] * 2
        + [jax.ShapeDtypeStruct((8, STATE), F32)],
        scratch_shapes=[
            pltpu.VMEM((2, rows // 2, rows // 2), F32),
            pltpu.VMEM((rows, width), F32),
        ],
        compiler_params=params(),
        cost_estimate=cost(8 * rows * rows * n * width, 12 * rows * n * width, rows * rows * heads),
        name="inner",
    )(proj, cum, cum_rows, step, x, gate)


def outer_kernel(first, proj, base, slope, *refs):
    states, (gated, squares) = refs[:-2], refs[-2:]
    c_rows = proj[:, STATE:]
    if first:
        total, states = states[0][...], states[1:]
    else:
        total = jnp.zeros(squares.shape, F32)
    for m, state in enumerate(states):
        read = jnp.dot(c_rows, state[...], preferred_element_type=F32)
        value = base[first + m] + slope[first + m] * read
        gated[m] = value
        square = value * value
        for k in range(value.shape[1] // STATE):
            total = total + square[:, k * STATE : (k + 1) * STATE]
    squares[...] = total


def outer_part(first, proj, base, slope, prior, states):
    n = len(states)
    _, rows, width = base.shape
    states = [*prior, *states]
    return pl.pallas_call(
        functools.partial(outer_kernel, first),
        in_specs=[VMEM] * (len(states) + 3),
        out_specs=[VMEM] * 2,
        out_shape=[
            jax.ShapeDtypeStruct((n, rows, width), F32),
            jax.ShapeDtypeStruct((rows, STATE), F32),
        ],
        compiler_params=params(),
        cost_estimate=cost(2 * rows * n * width * STATE, 12 * rows * n * width),
        name="outer",
    )(proj, base, slope, *states)


def norm_kernel(count, order, n, k, gain, *refs):
    place = position(len(order))
    parts, gated, (out, held, sems) = refs[:n], refs[n : n + k], refs[n + k :]
    total = parts[0][...]
    for part in parts[1:]:
        total = total + part[...]
    mean = jnp.sum(total, axis=1, keepdims=True) * (1.0 / count)
    scale = lax.rsqrt(mean + EPS)
    copies = []
    width = held.shape[2]
    pieces = [(ref, i) for ref in gated for i in range(ref.shape[0])]
    for at, (ref, i) in enumerate(pieces):
        cols = pl.ds(pl.multiple_of((place ^ order[at]) * width, width), width)
        held[at] = (ref[i] * scale * gain[:, cols]).astype(BF16)
        copy = pltpu.make_async_copy(held.at[at], out.at[:, cols], sems.at[at])
        copy.start()
        copies.append(copy)
    for copy in copies:
        copy.wait()


def normalise(count, order, parts, gated, gain):
    size = len(order)
    _, rows, width = gated[0].shape
    cols = size * width
    n, k = len(parts), len(gated)
    return pl.pallas_call(
        functools.partial(norm_kernel, count, order, n, k),
        in_specs=[VMEM] * (1 + n + k),
        out_specs=pl.BlockSpec(memory_space=pltpu.HBM),
        out_shape=jax.ShapeDtypeStruct((rows, cols), BF16),
        scratch_shapes=[pltpu.VMEM((size, rows, width), BF16), pltpu.SemaphoreType.DMA((size,))],
        compiler_params=params(),
        cost_estimate=cost(4 * rows * cols, 6 * rows * cols),
        name="norm",
    )(gain, *parts, *gated)


def swap(value, axis, mask):
    pairs = [(i, i ^ mask) for i in range(lax.axis_size(axis))]
    return lax.ppermute(value, axis, pairs)


def terms_of_sum(value, axis):
    mask = 1
    terms = [value]
    while mask < lax.axis_size(axis):
        if len(terms) > 1:
            terms = [sum(terms[1:], terms[0])]
        terms.append(swap(terms[0], axis, mask))
        mask *= 2
    return terms


def shards(hidden, weight, head_input, gate_input, step, rate, gain):
    heads = step.shape[1]
    devices = lax.axis_size("seq")
    size = 8
    while devices % size or heads % size or (heads // size * HEAD_DIM) % STATE:
        size //= 2
    groups = devices // size

    masks = [m for m in (1, 2, 4, 7, 3, 5, 6) if m < size]
    order = [0] + masks

    with jax.named_scope("projection"):
        parts = terms_of_sum(project(hidden, weight), "head")
    with jax.named_scope("decays"):
        weighted, cum, cum_rows, ends, step = decays(step.T, rate.reshape(1, heads), head_input)
    with jax.named_scope("states"):
        proj, *mine = fresh_states(size, parts, weighted, ends)
    with jax.named_scope("to_owners"):
        slices = [mine[0]] + [swap(mine[m], "seq", m) for m in masks]
    with jax.named_scope("groups"):
        total, decay = group_total(order, slices)
        up = [(i, (i + size) % devices) for i in range(devices)]
        before = jnp.zeros_like(total)
        for k in range(groups - 1):
            if k > 0:
                prior = jnp.where(lax.axis_index("seq") // size > 0, before.astype(F32), 0.0)
                sent = (prior * decay[:1] + total.astype(F32)).astype(BF16)
            else:
                sent = total
            before = lax.ppermute(sent, "seq", up)
        states, scales = local_states(order, slices)
    with jax.named_scope("inner"):
        base, slope, token = inside(order, proj, cum, cum_rows, step, head_input, gate_input)
    with jax.named_scope("from_owners"):
        outs = entering_states(states, scales, before, token)
        back = [outs[0]] + [swap(out, "seq", m) for m, out in zip(masks, outs[1:])]
    with jax.named_scope("outer"):
        cut = size // 2 + 1
        some, squares = outer_part(0, proj, base, slope, [], back[:cut])
        rest, squares = outer_part(cut, proj, base, slope, [squares], back[cut:])
    with jax.named_scope("norm"):
        count = head_input.shape[1] * lax.axis_size("head")
        sums = terms_of_sum(squares, "head")
        return normalise(count, order, sums, [some, rest], gain.reshape(1, -1))


def solution(mesh):
    in_specs = (
        P("seq", "head"),
        P(),
        P("seq", "head"),
        P("seq", "head"),
        P("seq", "head"),
        P("head"),
        P("head"),
    )
    return jax.shard_map(
        shards, mesh=mesh, in_specs=in_specs, out_specs=P("seq", "head"), check_vma=False
    )
```

```python
import functools

import jax
import jax.numpy as jnp
from jax import lax
from jax.experimental import pallas as pl
from jax.experimental.pallas import tpu as pltpu
from jax.sharding import PartitionSpec as P

HEAD_DIM = 64
STATE = 128
GROUP = 256
EPS = 1e-05
EXTRA = 8
LIMIT = 16 * 1024 * 1024
SEND_ORDER = (0, 1, 6, 2, 5, 4, 3, 7)
BACK_ORDER = (0, 1, 6, 2, 5, 4, 3, 7)
LOG2E = 1.4426950408889634

F32 = jnp.float32
BF16 = jnp.bfloat16
VMEM = pl.BlockSpec(memory_space=pltpu.VMEM)
SMEM = pl.BlockSpec(memory_space=pltpu.SMEM)


def in_hbm(value):
    return pltpu.with_memory_space_constraint(value, pltpu.HBM)


def params(limit=LIMIT):
    return pltpu.CompilerParams(vmem_limit_bytes=limit)


def cost(flops, moved, exps=0):
    return pl.CostEstimate(flops=flops, bytes_accessed=moved, transcendentals=exps)


def position(size):
    return lax.axis_index("seq") % size


def halves(value, count):
    terms = []
    for _ in range(count):
        term = value.astype(BF16)
        terms.append(term)
        value = value - term.astype(F32)
    return jnp.concatenate(terms, axis=1)


def picks(first_head, heads, lanes, width, count):
    row = lax.broadcasted_iota(jnp.int32, (heads, lanes), 0)
    col = lax.broadcasted_iota(jnp.int32, (heads, lanes), 1)
    pick = jnp.where(row == first_head + col // width, 1.0, 0.0).astype(BF16)
    return jnp.concatenate([pick] * count, axis=0)


def project_kernel(tiles, hidden, weight, out, rows_held, weight_held, sems):
    tile = hidden.shape[1] // tiles
    copies = []
    for k in range(tiles):
        row = pl.multiple_of(lax.axis_index("head") * hidden.shape[1] + k * tile, tile)
        pair = (
            pltpu.make_async_copy(
                hidden.at[:, pl.ds(k * tile, tile)], rows_held.at[k], sems.at[0, k]
            ),
            pltpu.make_async_copy(weight.at[pl.ds(row, tile), :], weight_held.at[k], sems.at[1, k]),
        )
        for copy in pair:
            copy.start()
        copies.append(pair)
    total = jnp.zeros(out.shape, F32)
    for k in range(tiles):
        for copy in copies[k]:
            copy.wait()
        total = total + jnp.dot(rows_held[k], weight_held[k], preferred_element_type=F32)
    out[...] = total


def project(hidden, weight):
    rows, depth = hidden.shape
    cols = weight.shape[1]
    tiles = 4
    tile = depth // tiles
    return pl.pallas_call(
        functools.partial(project_kernel, tiles),
        in_specs=[
            pl.BlockSpec(memory_space=pltpu.HBM),
            pl.BlockSpec(memory_space=pltpu.HBM),
        ],
        out_specs=VMEM,
        out_shape=jax.ShapeDtypeStruct((rows, cols), F32),
        scratch_shapes=[
            pltpu.VMEM((tiles, rows, tile), BF16),
            pltpu.VMEM((tiles, tile, cols), BF16),
            pltpu.SemaphoreType.DMA((2, tiles)),
        ],
        compiler_params=params(),
        cost_estimate=cost(2 * rows * depth * cols, 2 * rows * depth + 2 * depth * cols),
        name="project",
    )(in_hbm(hidden), in_hbm(weight))


def decay_kernel(tiles, step_rows, rate, x, weighted, cum, cum_rows, ends, step_out, held, sems):
    heads, rows = step_rows.shape
    cols = x.shape[1]
    lanes = cols // tiles
    copies = []
    for at in range(tiles):
        here = pl.ds(at * lanes, lanes)
        copies.append(pltpu.make_async_copy(x.at[:, here], held.at[at], sems.at[at]))
        copies[-1].start()
    step = step_rows[...].T
    step_out[...] = step
    log_decay = -step * rate[...]
    t = lax.broadcasted_iota(jnp.int32, (rows, rows), 0)
    s = lax.broadcasted_iota(jnp.int32, (rows, rows), 1)
    lower = jnp.where(s <= t, 1.0, 0.0).astype(BF16)
    parts = jnp.dot(lower, halves(log_decay, 3), preferred_element_type=F32)
    total = parts[:, :heads] + (parts[:, heads : 2 * heads] + parts[:, 2 * heads :])
    cum[...] = total
    cum_rows[...] = total.T
    last = total[rows - 1 :, :]
    factor = halves(jnp.exp(last - total) * step, 3)
    final = halves(jnp.broadcast_to(jnp.exp(last), (EXTRA, heads)), 3)
    both = jnp.concatenate([factor, final], axis=0)
    for at in range(tiles):
        here = slice(at * lanes, (at + 1) * lanes)
        pick = picks(at * (lanes // HEAD_DIM), heads, lanes, HEAD_DIM, 3)
        wide = jnp.dot(both, pick, preferred_element_type=F32)
        copies[at].wait()
        weighted[:, here] = (held[at].astype(F32) * wide[:rows]).astype(BF16)
        end = wide[rows:]
        high = end.astype(BF16).astype(F32)
        middle = (end - high).astype(BF16).astype(F32)
        low = end - high - middle
        row = lax.broadcasted_iota(jnp.int32, end.shape, 0)
        ends[:, here] = jnp.where(row == 0, high, jnp.where(row == 1, middle, low)).astype(BF16)


def decays(step_rows, rate, x):
    heads, rows = step_rows.shape
    cols = x.shape[1]
    tiles = max(1, cols // 1024)
    return pl.pallas_call(
        functools.partial(decay_kernel, tiles),
        in_specs=[VMEM, VMEM, pl.BlockSpec(memory_space=pltpu.HBM)],
        out_specs=[VMEM] * 6,
        out_shape=[
            jax.ShapeDtypeStruct((rows, cols), BF16),
            jax.ShapeDtypeStruct((rows, heads), F32),
            jax.ShapeDtypeStruct((heads, rows), F32),
            jax.ShapeDtypeStruct((EXTRA, cols), BF16),
            jax.ShapeDtypeStruct((rows, heads), F32),
            jax.ShapeDtypeStruct((tiles, rows, cols // tiles), BF16),
        ],
        scratch_shapes=[pltpu.SemaphoreType.DMA((tiles,))],
        compiler_params=params(),
        cost_estimate=cost(2 * rows * cols * 256, 4 * rows * cols, 2 * rows * heads),
        name="decays",
    )(step_rows, rate, in_hbm(x))


def fresh_kernel(n, *refs):
    parts, (weighted, ends, proj), slices = refs[:n], refs[n : n + 3], refs[n + 3 :]
    size = len(slices)
    place = position(size)
    total = parts[0][...]
    for part in parts[1:]:
        total = total + part[...]
    rounded = total.astype(BF16)
    proj[...] = rounded
    width = weighted.shape[1] // size
    b_rows = rounded[:, :STATE]
    for m in range(size):
        cols = pl.ds(pl.multiple_of((place ^ m) * width, width), width)
        state = lax.dot_general(
            b_rows, weighted[:, cols], (((0,), (0,)), ((), ())), preferred_element_type=F32
        )
        slices[m][:STATE, :] = state.astype(BF16)
        slices[m][STATE:, :] = ends[:, cols]


def fresh_states(size, parts, weighted, ends):
    rows, cols = weighted.shape
    width = cols // size
    n = len(parts)
    return pl.pallas_call(
        functools.partial(fresh_kernel, n),
        in_specs=[VMEM] * (n + 2),
        out_specs=[VMEM] * (1 + size),
        out_shape=[jax.ShapeDtypeStruct((rows, 2 * STATE), BF16)]
        + [jax.ShapeDtypeStruct((STATE + EXTRA, width), BF16)] * size,
        compiler_params=params(),
        cost_estimate=cost(2 * rows * cols * STATE, 4 * rows * cols),
        name="fresh",
    )(*parts, weighted, ends)


def gather_factors(order, slices, factors):
    place = position(len(order))
    for m, piece in zip(order, slices):
        tail = piece[STATE:, :].astype(F32)
        factors[place ^ m] = jnp.broadcast_to(tail[0:1] + (tail[1:2] + tail[2:3]), factors.shape[1:])


def total_kernel(order, *refs):
    place = position(len(order))
    slices, (token, out, decay, factors) = refs[:-4], refs[-4:]
    size = len(slices)
    gather_factors(order, slices, factors)
    product = jnp.ones(factors.shape[1:], F32)
    for j in reversed(range(size)):
        factor = factors[j]
        factors[j] = product
        product = product * factor
    decay[...] = product
    scales = [factors[place ^ m][:1] for m in order]
    step = 16
    for row in range(0, STATE, step):
        rows = slice(row, row + step)
        total = jnp.zeros((step, out.shape[1]), F32)
        for scale, piece in zip(scales, slices):
            total = total + scale * piece[rows, :].astype(F32)
        out[rows, :] = total.astype(BF16)


def group_total(order, slices, token):
    size = len(slices)
    width = slices[0].shape[1]
    return pl.pallas_call(
        functools.partial(total_kernel, order),
        in_specs=[VMEM] * (size + 1),
        out_specs=[VMEM] * 2,
        out_shape=[
            jax.ShapeDtypeStruct((STATE, width), BF16),
            jax.ShapeDtypeStruct((8, width), F32),
        ],
        scratch_shapes=[pltpu.VMEM((size, 8, width), F32)],
        compiler_params=params(),
        cost_estimate=cost(2 * size * STATE * width, 2 * size * STATE * width),
        name="total",
    )(*slices, token)


def local_kernel(order, back_order, *refs):
    place = position(len(order))
    slices, (states, scales, ordered, factors) = refs[:-4], refs[-4:]
    size = len(slices)
    gather_factors(order, slices, factors)
    for m, piece in zip(order, slices):
        ordered[place ^ m] = piece[:STATE, :]
    running = jnp.zeros(states.shape[1:], F32)
    product = jnp.ones(factors.shape[1:], F32)
    for j in range(size):
        at = jnp.int32(0)
        for i, m in enumerate(back_order):
            at = jnp.where(place ^ j == m, i, at)
        states[at] = running
        scales[at] = product
        running = running * factors[j][:1] + ordered[j].astype(F32)
        product = product * factors[j]


def local_states(order, back_order, slices):
    size = len(slices)
    width = slices[0].shape[1]
    return pl.pallas_call(
        functools.partial(local_kernel, order, back_order),
        in_specs=[VMEM] * size,
        out_specs=[VMEM] * 2,
        out_shape=[
            jax.ShapeDtypeStruct((size, STATE, width), F32),
            jax.ShapeDtypeStruct((size, 8, width), F32),
        ],
        scratch_shapes=[
            pltpu.VMEM((size, STATE, width), BF16),
            pltpu.VMEM((size, 8, width), F32),
        ],
        compiler_params=params(),
        cost_estimate=cost(2 * size * STATE * width, 6 * size * STATE * width),
        name="local",
    )(*slices)


def enter_kernel(states, scales, before, token, *outs):
    group = lax.axis_index("seq") // len(outs)
    entering = jnp.where(group > 0, before[...].astype(F32), 0.0)
    for m, out in enumerate(outs):
        out[...] = (entering * scales[m][:1] + states[m]).astype(BF16)


def entering_states(states, scales, before, token):
    size, _, width = states.shape
    return pl.pallas_call(
        enter_kernel,
        in_specs=[VMEM] * 4,
        out_specs=[VMEM] * size,
        out_shape=[jax.ShapeDtypeStruct((STATE, width), BF16)] * size,
        compiler_params=params(),
        cost_estimate=cost(2 * size * STATE * width, 6 * size * STATE * width),
        name="entering",
    )(states, scales, before, token)


def inner_kernel(
    size, order, proj, cum, cum_rows, step, x, gate, base, slope, token, scores, mixed, held, sems
):
    rows, heads = cum.shape
    width = base.shape[2]
    here = width // HEAD_DIM
    half = rows // 2
    place = position(size)

    def gate_copy(at):
        cols = pl.ds(pl.multiple_of((place ^ entry(order, at)) * width, width), width)
        return pltpu.make_async_copy(gate.at[:, cols], held.at[at], sems.at[at])

    for at in range(len(order)):
        gate_copy(at).start()
    all_scores = lax.dot_general(
        proj[:, STATE:], proj[:, :STATE], (((1,), (1,)), ((), ())), preferred_element_type=F32
    )
    t = lax.broadcasted_iota(jnp.int32, (half, half), 0)
    s = lax.broadcasted_iota(jnp.int32, (half, half), 1)
    scores[0] = jnp.where(s <= t, all_scores[:half, :half], 0.0)
    scores[1] = jnp.where(s <= t, all_scores[half:, half:], 0.0)
    lower = all_scores[half:, :half].astype(BF16)
    total = cum[...]
    middle = total[half - 1 : half, :]
    grown = jnp.exp(total)
    later = jnp.concatenate(
        [jnp.exp(middle - total[:half]) * step[:half, :], jnp.exp(total[half:] - middle)], axis=0
    )
    per_head = jnp.concatenate([halves(value, 3) for value in (step[...], grown, later)], axis=0)
    parts = halves(total * LOG2E, 3)
    token[...] = jnp.zeros(token.shape, F32)

    def one(at, carry):
        owner = place ^ entry(order, at)
        first = owner * here
        wide = jnp.dot(per_head, picks(first, heads, width, HEAD_DIM, 3), preferred_element_type=F32)
        columns = jnp.dot(
            parts, picks(first, heads, here * half, half, 3), preferred_element_type=F32
        )
        each = x.shape[2] // width
        piece = pl.ds(pl.multiple_of(owner % each * width, width), width)
        values = x[owner // each, :, piece].astype(F32)
        scaled = (values * wide[:rows]).astype(BF16)
        early = (values[:half] * wide[2 * rows : 2 * rows + half]).astype(BF16)
        cross = jnp.dot(lower, early, preferred_element_type=F32) * wide[2 * rows + half :]
        for k in range(here):
            line = cum_rows[pl.ds(first + k, 1), :] * LOG2E
            mine = slice(k * HEAD_DIM, (k + 1) * HEAD_DIM)
            for i in range(2):
                span = slice(i * half, (i + 1) * half)
                gap = columns[span, k * half : (k + 1) * half] - line[:, span]
                block = (scores[i] * jnp.exp2(jnp.minimum(gap, 0.0))).astype(BF16)
                mixed[span, mine] = jnp.dot(block, scaled[span, mine], preferred_element_type=F32)
        gate_copy(at).wait()
        g = held[at].astype(F32)
        silu = g / (1.0 + jnp.exp(-g))
        base[at, :half, :] = mixed[:half, :] * silu[:half]
        base[at, half:, :] = (mixed[half:, :] + cross) * silu[half:]
        slope[at] = wide[rows : 2 * rows] * silu
        return carry

    lax.fori_loop(0, base.shape[0], one, 0)


def entry(order, at):
    value = jnp.int32(order[0])
    for i, m in enumerate(order):
        value = jnp.where(at == i, m, value)
    return value


def inside(size, order, proj, cum, cum_rows, step, x, gate):
    rows, heads = step.shape
    n = len(order)
    width = gate.shape[1] // size
    return pl.pallas_call(
        functools.partial(inner_kernel, size, order),
        in_specs=[VMEM] * 5 + [pl.BlockSpec(memory_space=pltpu.HBM)],
        out_specs=[VMEM] * 3,
        out_shape=[jax.ShapeDtypeStruct((n, rows, width), F32)] * 2
        + [jax.ShapeDtypeStruct((8, STATE), F32)],
        scratch_shapes=[
            pltpu.VMEM((2, rows // 2, rows // 2), F32),
            pltpu.VMEM((rows, width), F32),
            pltpu.VMEM((n, rows, width), BF16),
            pltpu.SemaphoreType.DMA((n,)),
        ],
        compiler_params=params(),
        cost_estimate=cost(8 * rows * rows * n * width, 12 * rows * n * width, rows * rows * heads),
        name="inner",
    )(proj, cum, cum_rows, step, x, in_hbm(gate))


def outer_kernel(prior, proj, base, slope, *refs):
    states, (gated, squares) = refs[:-2], refs[-2:]
    c_rows = proj[:, STATE:]
    if prior:
        total, states = states[0][...], states[1:]
    else:
        total = jnp.zeros(squares.shape, F32)
    for m, state in enumerate(states):
        read = jnp.dot(c_rows, state[...], preferred_element_type=F32)
        value = base[m] + slope[m] * read
        gated[m] = value
        square = value * value
        for k in range(value.shape[1] // STATE):
            total = total + square[:, k * STATE : (k + 1) * STATE]
    squares[...] = total


def outer_part(proj, base, slope, prior, states):
    n = len(states)
    _, rows, width = base.shape
    states = [*prior, *states]
    return pl.pallas_call(
        functools.partial(outer_kernel, len(prior)),
        in_specs=[VMEM] * (len(states) + 3),
        out_specs=[VMEM] * 2,
        out_shape=[
            jax.ShapeDtypeStruct((n, rows, width), F32),
            jax.ShapeDtypeStruct((rows, STATE), F32),
        ],
        compiler_params=params(),
        cost_estimate=cost(2 * rows * n * width * STATE, 12 * rows * n * width),
        name="outer",
    )(proj, base, slope, *states)


def norm_kernel(count, order, n, k, gain, *refs):
    place = position(len(order))
    parts, gated, (out, held, sems) = refs[:n], refs[n : n + k], refs[n + k :]
    total = parts[0][...]
    for part in parts[1:]:
        total = total + part[...]
    mean = jnp.sum(total, axis=1, keepdims=True) * (1.0 / count)
    scale = lax.rsqrt(mean + EPS)
    copies = []
    width = held.shape[2]
    pieces = [(ref, i) for ref in gated for i in range(ref.shape[0])]
    for at, (ref, i) in enumerate(pieces):
        cols = pl.ds(pl.multiple_of((place ^ order[at]) * width, width), width)
        held[at] = (ref[i] * scale * gain[:, cols]).astype(BF16)
        copy = pltpu.make_async_copy(held.at[at], out.at[:, cols], sems.at[at])
        copy.start()
        copies.append(copy)
    for copy in copies:
        copy.wait()


def normalise(count, order, parts, gated, gain):
    size = len(order)
    _, rows, width = gated[0].shape
    cols = size * width
    n, k = len(parts), len(gated)
    return pl.pallas_call(
        functools.partial(norm_kernel, count, order, n, k),
        in_specs=[VMEM] * (1 + n + k),
        out_specs=pl.BlockSpec(memory_space=pltpu.HBM),
        out_shape=jax.ShapeDtypeStruct((rows, cols), BF16),
        scratch_shapes=[pltpu.VMEM((size, rows, width), BF16), pltpu.SemaphoreType.DMA((size,))],
        compiler_params=params(),
        cost_estimate=cost(4 * rows * cols, 6 * rows * cols),
        name="norm",
    )(gain, *parts, *gated)


def swap(value, axis, mask):
    pairs = [(i, i ^ mask) for i in range(lax.axis_size(axis))]
    return lax.ppermute(value, axis, pairs)


def terms_of_sum(value, axis):
    mask = 1
    terms = [value]
    while mask < lax.axis_size(axis):
        if len(terms) > 1:
            terms = [sum(terms[1:], terms[0])]
        terms.append(swap(terms[0], axis, mask))
        mask *= 2
    return terms


def shards(hidden, weight, head_input, gate_input, step, rate, gain):
    heads = step.shape[1]
    devices = lax.axis_size("seq")
    size = 8
    while devices % size or heads % size or (heads // size * HEAD_DIM) % STATE:
        size //= 2
    groups = devices // size

    order = [m for m in SEND_ORDER if m < size]
    back_order = [m for m in BACK_ORDER if m < size]

    with jax.named_scope("projection"):
        parts = terms_of_sum(project(hidden, weight), "head")
    with jax.named_scope("decays"):
        weighted, cum, cum_rows, ends, step, x = decays(
            step.T, rate.reshape(1, heads), head_input
        )
    with jax.named_scope("states"):
        proj, *mine = fresh_states(size, parts, weighted, ends)
    with jax.named_scope("to_owners"):
        slices = [mine[0]] + [swap(mine[m], "seq", m) for m in order[1:]]
    with jax.named_scope("inner"):
        cut = size // 2 + 1
        given = (proj, cum, cum_rows, step, x, gate_input)
        *early, token = inside(size, back_order[:cut], *given)
        *late, late_token = inside(size, back_order[cut:], *given)
    with jax.named_scope("groups"):
        total, decay = group_total(order, slices, token)
        up = [(i, (i + size) % devices) for i in range(devices)]
        before = jnp.zeros_like(total)
        for k in range(groups - 1):
            if k > 0:
                prior = jnp.where(lax.axis_index("seq") // size > 0, before.astype(F32), 0.0)
                sent = (prior * decay[:1] + total.astype(F32)).astype(BF16)
            else:
                sent = total
            before = lax.ppermute(sent, "seq", up)
        states, scales = local_states(order, back_order, slices)
    with jax.named_scope("from_owners"):
        outs = entering_states(states, scales, before, late_token)
        back = [outs[0]] + [swap(out, "seq", m) for m, out in zip(back_order[1:], outs[1:])]
    with jax.named_scope("outer"):
        some, squares = outer_part(proj, *early, [], back[:cut])
        rest, squares = outer_part(proj, *late, [squares], back[cut:])
    with jax.named_scope("norm"):
        count = head_input.shape[1] * lax.axis_size("head")
        sums = terms_of_sum(squares, "head")
        return normalise(count, back_order, sums, [some, rest], gain.reshape(1, -1))


def solution(mesh):
    in_specs = (
        P("seq", "head"),
        P(),
        P("seq", "head"),
        P("seq", "head"),
        P("seq", "head"),
        P("head"),
        P("head"),
    )
    return jax.shard_map(
        shards, mesh=mesh, in_specs=in_specs, out_specs=P("seq", "head"), check_vma=False
    )
```

```python
import functools

import jax
import jax.numpy as jnp
from jax import lax
from jax.experimental import pallas as pl
from jax.experimental.pallas import tpu as pltpu
from jax.sharding import PartitionSpec as P

HEAD_DIM = 64
STATE = 128
GROUP = 256
EPS = 1e-05
EXTRA = 8
LIMIT = 16 * 1024 * 1024
SEND_ORDER = (0, 1, 6, 2, 5, 4, 3, 7)
BACK_ORDER = (0, 1, 6, 2, 5, 4, 3, 7)
LOG2E = 1.4426950408889634

F32 = jnp.float32
BF16 = jnp.bfloat16
VMEM = pl.BlockSpec(memory_space=pltpu.VMEM)
SMEM = pl.BlockSpec(memory_space=pltpu.SMEM)


def in_hbm(value):
    return pltpu.with_memory_space_constraint(value, pltpu.HBM)


def params(limit=LIMIT):
    return pltpu.CompilerParams(vmem_limit_bytes=limit)


def cost(flops, moved, exps=0):
    return pl.CostEstimate(flops=flops, bytes_accessed=moved, transcendentals=exps)


def turns(order, size):
    last = size - 1
    return [(m, m ^ last if 0 < m < last else m) for m in order if m < size]


def partner(pair):
    even, odd = pair
    return even + (lax.axis_index("head") % 2) * (odd - even)


def position(size):
    return lax.axis_index("seq") % size


def halves(value, count):
    terms = []
    for _ in range(count):
        term = value.astype(BF16)
        terms.append(term)
        value = value - term.astype(F32)
    return jnp.concatenate(terms, axis=1)


def picks(first_head, heads, lanes, width, count):
    row = lax.broadcasted_iota(jnp.int32, (heads, lanes), 0)
    col = lax.broadcasted_iota(jnp.int32, (heads, lanes), 1)
    pick = jnp.where(row == first_head + col // width, 1.0, 0.0).astype(BF16)
    return jnp.concatenate([pick] * count, axis=0)


def project_kernel(tiles, hidden, weight, out, rows_held, weight_held, sems):
    tile = hidden.shape[1] // tiles
    copies = []
    for k in range(tiles):
        row = pl.multiple_of(lax.axis_index("head") * hidden.shape[1] + k * tile, tile)
        pair = (
            pltpu.make_async_copy(
                hidden.at[:, pl.ds(k * tile, tile)], rows_held.at[k], sems.at[0, k]
            ),
            pltpu.make_async_copy(weight.at[pl.ds(row, tile), :], weight_held.at[k], sems.at[1, k]),
        )
        for copy in pair:
            copy.start()
        copies.append(pair)
    total = jnp.zeros(out.shape, F32)
    for k in range(tiles):
        for copy in copies[k]:
            copy.wait()
        total = total + jnp.dot(rows_held[k], weight_held[k], preferred_element_type=F32)
    out[...] = total


def project(hidden, weight):
    rows, depth = hidden.shape
    cols = weight.shape[1]
    tiles = 2
    tile = depth // tiles
    return pl.pallas_call(
        functools.partial(project_kernel, tiles),
        in_specs=[
            pl.BlockSpec(memory_space=pltpu.HBM),
            pl.BlockSpec(memory_space=pltpu.HBM),
        ],
        out_specs=VMEM,
        out_shape=jax.ShapeDtypeStruct((rows, cols), F32),
        scratch_shapes=[
            pltpu.VMEM((tiles, rows, tile), BF16),
            pltpu.VMEM((tiles, tile, cols), BF16),
            pltpu.SemaphoreType.DMA((2, tiles)),
        ],
        compiler_params=params(),
        cost_estimate=cost(2 * rows * depth * cols, 2 * rows * depth + 2 * depth * cols),
        name="project",
    )(in_hbm(hidden), in_hbm(weight))


def decay_kernel(tiles, step_rows, rate, x, weighted, cum, cum_rows, ends, step_out, held, sems):
    heads, rows = step_rows.shape
    cols = x.shape[1]
    lanes = cols // tiles
    copies = []
    for at in range(tiles):
        here = pl.ds(at * lanes, lanes)
        copies.append(pltpu.make_async_copy(x.at[:, here], held.at[at], sems.at[at]))
        copies[-1].start()
    step = step_rows[...].T
    step_out[...] = step
    log_decay = -step * rate[...]
    t = lax.broadcasted_iota(jnp.int32, (rows, rows), 0)
    s = lax.broadcasted_iota(jnp.int32, (rows, rows), 1)
    lower = jnp.where(s <= t, 1.0, 0.0).astype(BF16)
    parts = jnp.dot(lower, halves(log_decay, 3), preferred_element_type=F32)
    total = parts[:, :heads] + (parts[:, heads : 2 * heads] + parts[:, 2 * heads :])
    cum[...] = total
    cum_rows[...] = total.T
    last = total[rows - 1 :, :]
    factor = halves(jnp.exp(last - total) * step, 3)
    final = halves(jnp.broadcast_to(jnp.exp(last), (EXTRA, heads)), 3)
    both = jnp.concatenate([factor, final], axis=0)
    wides = []
    for at in range(tiles):
        here = slice(at * lanes, (at + 1) * lanes)
        pick = picks(at * (lanes // HEAD_DIM), heads, lanes, HEAD_DIM, 3)
        wide = jnp.dot(both, pick, preferred_element_type=F32)
        wides.append(wide[:rows])
        end = wide[rows:]
        high = end.astype(BF16).astype(F32)
        middle = (end - high).astype(BF16).astype(F32)
        low = end - high - middle
        row = lax.broadcasted_iota(jnp.int32, end.shape, 0)
        ends[:, here] = jnp.where(row == 0, high, jnp.where(row == 1, middle, low)).astype(BF16)
    for at in range(tiles):
        copies[at].wait()
        here = slice(at * lanes, (at + 1) * lanes)
        weighted[:, here] = (held[at].astype(F32) * wides[at]).astype(BF16)


def decays(step_rows, rate, x):
    heads, rows = step_rows.shape
    cols = x.shape[1]
    tiles = max(1, cols // 1024)
    return pl.pallas_call(
        functools.partial(decay_kernel, tiles),
        in_specs=[VMEM, VMEM, pl.BlockSpec(memory_space=pltpu.HBM)],
        out_specs=[VMEM] * 6,
        out_shape=[
            jax.ShapeDtypeStruct((rows, cols), BF16),
            jax.ShapeDtypeStruct((rows, heads), F32),
            jax.ShapeDtypeStruct((heads, rows), F32),
            jax.ShapeDtypeStruct((EXTRA, cols), BF16),
            jax.ShapeDtypeStruct((rows, heads), F32),
            jax.ShapeDtypeStruct((tiles, rows, cols // tiles), BF16),
        ],
        scratch_shapes=[pltpu.SemaphoreType.DMA((tiles,))],
        compiler_params=params(),
        cost_estimate=cost(2 * rows * cols * 256, 4 * rows * cols, 2 * rows * heads),
        name="decays",
    )(step_rows, rate, in_hbm(x))


def fresh_kernel(order, n, *refs):
    parts, (weighted, ends, proj), slices = refs[:n], refs[n : n + 3], refs[n + 3 :]
    size = len(slices)
    place = position(size)
    total = parts[0][...]
    for part in parts[1:]:
        total = total + part[...]
    rounded = total.astype(BF16)
    proj[...] = rounded
    width = weighted.shape[1] // size
    b_rows = rounded[:, :STATE]
    for m, pair in enumerate(order):
        cols = pl.ds(pl.multiple_of((place ^ partner(pair)) * width, width), width)
        state = lax.dot_general(
            b_rows, weighted[:, cols], (((0,), (0,)), ((), ())), preferred_element_type=F32
        )
        slices[m][:STATE, :] = state.astype(BF16)
        slices[m][STATE:, :] = ends[:, cols]


def fresh_states(order, parts, weighted, ends):
    rows, cols = weighted.shape
    size = len(order)
    width = cols // size
    n = len(parts)
    return pl.pallas_call(
        functools.partial(fresh_kernel, order, n),
        in_specs=[VMEM] * (n + 2),
        out_specs=[VMEM] * (1 + size),
        out_shape=[jax.ShapeDtypeStruct((rows, 2 * STATE), BF16)]
        + [jax.ShapeDtypeStruct((STATE + EXTRA, width), BF16)] * size,
        compiler_params=params(),
        cost_estimate=cost(2 * rows * cols * STATE, 4 * rows * cols),
        name="fresh",
    )(*parts, weighted, ends)


def gather_factors(order, slices, factors):
    place = position(len(order))
    for pair, piece in zip(order, slices):
        tail = piece[STATE:, :].astype(F32)
        factors[place ^ partner(pair)] = jnp.broadcast_to(tail[0:1] + (tail[1:2] + tail[2:3]), factors.shape[1:])


def total_kernel(order, *refs):
    place = position(len(order))
    slices, (token, out, decay, factors) = refs[:-4], refs[-4:]
    size = len(slices)
    gather_factors(order, slices, factors)
    product = jnp.ones(factors.shape[1:], F32)
    for j in reversed(range(size)):
        factor = factors[j]
        factors[j] = product
        product = product * factor
    decay[...] = product
    scales = [factors[place ^ partner(pair)][:1] for pair in order]
    step = 16
    for row in range(0, STATE, step):
        rows = slice(row, row + step)
        total = jnp.zeros((step, out.shape[1]), F32)
        for scale, piece in zip(scales, slices):
            total = total + scale * piece[rows, :].astype(F32)
        out[rows, :] = total.astype(BF16)


def group_total(order, slices, token):
    size = len(slices)
    width = slices[0].shape[1]
    return pl.pallas_call(
        functools.partial(total_kernel, order),
        in_specs=[VMEM] * (size + 1),
        out_specs=[VMEM] * 2,
        out_shape=[
            jax.ShapeDtypeStruct((STATE, width), BF16),
            jax.ShapeDtypeStruct((8, width), F32),
        ],
        scratch_shapes=[pltpu.VMEM((size, 8, width), F32)],
        compiler_params=params(),
        cost_estimate=cost(2 * size * STATE * width, 2 * size * STATE * width),
        name="total",
    )(*slices, token)


def local_kernel(order, back_order, *refs):
    place = position(len(order))
    slices, (states, scales, ordered, factors) = refs[:-4], refs[-4:]
    size = len(slices)
    gather_factors(order, slices, factors)
    for pair, piece in zip(order, slices):
        ordered[place ^ partner(pair)] = piece[:STATE, :]
    running = jnp.zeros(states.shape[1:], F32)
    product = jnp.ones(factors.shape[1:], F32)
    for j in range(size):
        at = jnp.int32(0)
        for i, pair in enumerate(back_order):
            at = jnp.where(place ^ j == partner(pair), i, at)
        states[at] = running
        scales[at] = product
        running = running * factors[j][:1] + ordered[j].astype(F32)
        product = product * factors[j]


def local_states(order, back_order, slices):
    size = len(slices)
    width = slices[0].shape[1]
    return pl.pallas_call(
        functools.partial(local_kernel, order, back_order),
        in_specs=[VMEM] * size,
        out_specs=[VMEM] * 2,
        out_shape=[
            jax.ShapeDtypeStruct((size, STATE, width), F32),
            jax.ShapeDtypeStruct((size, 8, width), F32),
        ],
        scratch_shapes=[
            pltpu.VMEM((size, STATE, width), BF16),
            pltpu.VMEM((size, 8, width), F32),
        ],
        compiler_params=params(),
        cost_estimate=cost(2 * size * STATE * width, 6 * size * STATE * width),
        name="local",
    )(*slices)


def enter_kernel(states, scales, before, token, *outs):
    group = lax.axis_index("seq") // len(outs)
    entering = jnp.where(group > 0, before[...].astype(F32), 0.0)
    for m, out in enumerate(outs):
        out[...] = (entering * scales[m][:1] + states[m]).astype(BF16)


def entering_states(states, scales, before, token):
    size, _, width = states.shape
    return pl.pallas_call(
        enter_kernel,
        in_specs=[VMEM] * 4,
        out_specs=[VMEM] * size,
        out_shape=[jax.ShapeDtypeStruct((STATE, width), BF16)] * size,
        compiler_params=params(),
        cost_estimate=cost(2 * size * STATE * width, 6 * size * STATE * width),
        name="entering",
    )(states, scales, before, token)


def inner_kernel(size, order, leads, proj, cum, cum_rows, step, x, gate, base, slope, *refs):
    if leads:
        token, held, scores, mixed, sems = refs
    else:
        token, scores, mixed = refs
    rows, heads = cum.shape
    width = base.shape[2]
    here = width // HEAD_DIM
    half = rows // 2
    place = position(size)

    def gate_copy(at):
        cols = pl.ds(pl.multiple_of((place ^ entry(order, at)) * width, width), width)
        return pltpu.make_async_copy(gate.at[:, cols], held.at[at], sems.at[at])

    if leads:
        for at in range(len(order)):
            gate_copy(at).start()
    all_scores = lax.dot_general(
        proj[:, STATE:], proj[:, :STATE], (((1,), (1,)), ((), ())), preferred_element_type=F32
    )
    t = lax.broadcasted_iota(jnp.int32, (half, half), 0)
    s = lax.broadcasted_iota(jnp.int32, (half, half), 1)
    scores[0] = jnp.where(s <= t, all_scores[:half, :half], 0.0)
    scores[1] = jnp.where(s <= t, all_scores[half:, half:], 0.0)
    lower = all_scores[half:, :half].astype(BF16)
    total = cum[...]
    middle = total[half - 1 : half, :]
    grown = jnp.exp(total)
    later = jnp.concatenate(
        [jnp.exp(middle - total[:half]) * step[:half, :], jnp.exp(total[half:] - middle)], axis=0
    )
    per_head = jnp.concatenate([halves(value, 3) for value in (step[...], grown, later)], axis=0)
    parts = halves(total * LOG2E, 3)
    token[...] = jnp.zeros(token.shape, F32)
    lane = lax.broadcasted_iota(jnp.int32, (half, 2 * HEAD_DIM), 1)
    first_head = jnp.where(lane < HEAD_DIM, 1.0, 0.0).astype(BF16)
    second_head = jnp.where(lane < HEAD_DIM, 0.0, 1.0).astype(BF16)

    def one(at, carry):
        owner = place ^ entry(order if leads else order[-base.shape[0] :], at)
        first = owner * here
        wide = jnp.dot(per_head, picks(first, heads, width, HEAD_DIM, 3), preferred_element_type=F32)
        columns = jnp.dot(
            parts, picks(first, heads, here * half, half, 3), preferred_element_type=F32
        )
        each = x.shape[2] // width
        piece = pl.ds(pl.multiple_of(owner % each * width, width), width)
        values = x[owner // each, :, piece].astype(F32)
        scaled = (values * wide[:rows]).astype(BF16)
        early = (values[:half] * wide[2 * rows : 2 * rows + half]).astype(BF16)
        cross = jnp.dot(lower, early, preferred_element_type=F32) * wide[2 * rows + half :]
        for k in range(0, here, 2):
            pair = slice(k * HEAD_DIM, (k + 2) * HEAD_DIM)
            lines = [cum_rows[pl.ds(first + k + n, 1), :] * LOG2E for n in range(2)]
            for i in range(2):
                span = slice(i * half, (i + 1) * half)
                blocks = []
                for n, line in enumerate(lines):
                    gap = columns[span, (k + n) * half : (k + n + 1) * half] - line[:, span]
                    blocks.append((scores[i] * jnp.exp2(jnp.minimum(gap, 0.0))).astype(BF16))
                both = scaled[span, pair]
                mixed[span, pair] = jnp.dot(
                    jnp.concatenate(blocks, axis=1),
                    jnp.concatenate([both * first_head, both * second_head], axis=0),
                    preferred_element_type=F32,
                )
        if leads:
            gate_copy(at).wait()
            g = held[at].astype(F32)
        else:
            g = gate[at + len(order) - base.shape[0]].astype(F32)
        silu = g / (1.0 + jnp.exp(-g))
        base[at, :half, :] = mixed[:half, :] * silu[:half]
        base[at, half:, :] = (mixed[half:, :] + cross) * silu[half:]
        slope[at] = wide[rows : 2 * rows] * silu
        return carry

    lax.fori_loop(0, base.shape[0], one, 0)
    if leads:
        for at in range(base.shape[0], len(order)):
            gate_copy(at).wait()


def entry(order, at):
    value = jnp.int32(0)
    for i, pair in enumerate(order):
        value = jnp.where(at == i, partner(pair), value)
    return value


def inside(order, start, stop, proj, cum, cum_rows, step, x, gate):
    rows, heads = step.shape
    size, n = len(order), stop - start
    first = start == 0
    width = heads // size * HEAD_DIM
    held = [jax.ShapeDtypeStruct((size, rows, width), BF16)] if first else []
    sems = [pltpu.SemaphoreType.DMA((size,))] if first else []
    return pl.pallas_call(
        functools.partial(inner_kernel, size, order if first else order[:stop], first),
        in_specs=[VMEM] * 5 + [pl.BlockSpec(memory_space=pltpu.HBM) if first else VMEM],
        out_specs=[VMEM] * (3 + len(held)),
        out_shape=[jax.ShapeDtypeStruct((n, rows, width), F32)] * 2
        + [jax.ShapeDtypeStruct((8, STATE), F32)]
        + held,
        scratch_shapes=[
            pltpu.VMEM((2, rows // 2, rows // 2), F32),
            pltpu.VMEM((rows, width), F32),
        ]
        + sems,
        compiler_params=params(),
        cost_estimate=cost(8 * rows * rows * n * width, 12 * rows * n * width, rows * rows * heads),
        name="inner",
    )(proj, cum, cum_rows, step, x, in_hbm(gate) if first else gate)


def outer_kernel(prior, proj, base, slope, *refs):
    states, (gated, squares) = refs[:-2], refs[-2:]
    c_rows = proj[:, STATE:]
    if prior:
        total, states = states[0][...], states[1:]
    else:
        total = jnp.zeros(squares.shape, F32)
    for m, state in enumerate(states):
        read = jnp.dot(c_rows, state[...], preferred_element_type=F32)
        value = base[m] + slope[m] * read
        gated[m] = value
        square = value * value
        for k in range(value.shape[1] // STATE):
            total = total + square[:, k * STATE : (k + 1) * STATE]
    squares[...] = total


def outer_part(proj, base, slope, prior, states):
    n = len(states)
    _, rows, width = base.shape
    states = [*prior, *states]
    return pl.pallas_call(
        functools.partial(outer_kernel, len(prior)),
        in_specs=[VMEM] * (len(states) + 3),
        out_specs=[VMEM] * 2,
        out_shape=[
            jax.ShapeDtypeStruct((n, rows, width), F32),
            jax.ShapeDtypeStruct((rows, STATE), F32),
        ],
        compiler_params=params(),
        cost_estimate=cost(2 * rows * n * width * STATE, 12 * rows * n * width),
        name="outer",
    )(proj, base, slope, *states)


def norm_kernel(count, order, n, k, gain, *refs):
    place = position(len(order))
    parts, gated, (out, held, sems) = refs[:n], refs[n : n + k], refs[n + k :]
    total = parts[0][...]
    for part in parts[1:]:
        total = total + part[...]
    mean = jnp.sum(total, axis=1, keepdims=True) * (1.0 / count)
    scale = lax.rsqrt(mean + EPS)
    copies = []
    width = held.shape[2]
    pieces = [(ref, i) for ref in gated for i in range(ref.shape[0])]
    for at, (ref, i) in enumerate(pieces):
        cols = pl.ds(pl.multiple_of((place ^ partner(order[at])) * width, width), width)
        held[at] = (ref[i] * scale * gain[:, cols]).astype(BF16)
        copy = pltpu.make_async_copy(held.at[at], out.at[:, cols], sems.at[at])
        copy.start()
        copies.append(copy)
    for copy in copies:
        copy.wait()


def normalise(count, order, parts, gated, gain):
    size = len(order)
    _, rows, width = gated[0].shape
    cols = size * width
    n, k = len(parts), len(gated)
    return pl.pallas_call(
        functools.partial(norm_kernel, count, order, n, k),
        in_specs=[VMEM] * (1 + n + k),
        out_specs=pl.BlockSpec(memory_space=pltpu.HBM),
        out_shape=jax.ShapeDtypeStruct((rows, cols), BF16),
        scratch_shapes=[pltpu.VMEM((size, rows, width), BF16), pltpu.SemaphoreType.DMA((size,))],
        compiler_params=params(),
        cost_estimate=cost(4 * rows * cols, 6 * rows * cols),
        name="norm",
    )(gain, *parts, *gated)


def swap(value, axis, mask):
    pairs = [(i, i ^ mask) for i in range(lax.axis_size(axis))]
    return lax.ppermute(value, axis, pairs)


def exchange(value, pair):
    count = lax.axis_size("head")
    pairs = [
        (i * count + c, (i ^ pair[c % 2]) * count + c)
        for i in range(lax.axis_size("seq"))
        for c in range(count)
    ]
    return lax.ppermute(value, ("seq", "head"), pairs)


def terms_of_sum(value, axis):
    mask = 1
    terms = [value]
    while mask < lax.axis_size(axis):
        if len(terms) > 1:
            terms = [sum(terms[1:], terms[0])]
        terms.append(swap(terms[0], axis, mask))
        mask *= 2
    return terms


def shards(hidden, weight, head_input, gate_input, step, rate, gain):
    heads = step.shape[1]
    devices = lax.axis_size("seq")
    size = 8
    while devices % size or heads % size or (heads // size * HEAD_DIM) % STATE:
        size //= 2
    groups = devices // size

    order = turns(SEND_ORDER, size)
    back_order = turns(BACK_ORDER, size)

    with jax.named_scope("projection"):
        parts = terms_of_sum(project(hidden, weight), "head")
    with jax.named_scope("decays"):
        weighted, cum, cum_rows, ends, step, x = decays(
            step.T, rate.reshape(1, heads), head_input
        )
    with jax.named_scope("states"):
        proj, *mine = fresh_states(order, parts, weighted, ends)
    with jax.named_scope("to_owners"):
        slices = [mine[0]] + [exchange(part, pair) for pair, part in zip(order[1:], mine[1:])]
    with jax.named_scope("inner"):
        ends_at = sorted({size // 2 + 1, size})
        bounds = list(zip([0] + ends_at[:-1], ends_at))
        inner, gate = [], gate_input
        for a, b in bounds:
            *made, gate = [*inside(back_order, a, b, proj, cum, cum_rows, step, x, gate), gate][:4]
            inner.append(made)
    with jax.named_scope("groups"):
        total, decay = group_total(order, slices, inner[0][2])
        up = [(i, (i + size) % devices) for i in range(devices)]
        before = jnp.zeros_like(total)
        for k in range(groups - 1):
            if k > 0:
                prior = jnp.where(lax.axis_index("seq") // size > 0, before.astype(F32), 0.0)
                sent = (prior * decay[:1] + total.astype(F32)).astype(BF16)
            else:
                sent = total
            before = lax.ppermute(sent, "seq", up)
        states, scales = local_states(order, back_order, slices)
    with jax.named_scope("from_owners"):
        outs = entering_states(states, scales, before, inner[min(1, len(inner) - 1)][2])
        back = [outs[0]] + [exchange(out, pair) for pair, out in zip(back_order[1:], outs[1:])]
    with jax.named_scope("outer"):
        gated, squares = [], []
        for (a, b), (base, slope, _) in zip(bounds, inner):
            value, total = outer_part(proj, base, slope, squares, back[a:b])
            gated.append(value)
            squares = [total]
    with jax.named_scope("norm"):
        count = head_input.shape[1] * lax.axis_size("head")
        sums = terms_of_sum(squares[0], "head")
        return normalise(count, back_order, sums, gated, gain.reshape(1, -1))


def solution(mesh):
    in_specs = (
        P("seq", "head"),
        P(),
        P("seq", "head"),
        P("seq", "head"),
        P("seq", "head"),
        P("head"),
        P("head"),
    )
    return jax.shard_map(
        shards, mesh=mesh, in_specs=in_specs, out_specs=P("seq", "head"), check_vma=False
    )
```

```python
import functools

import jax
import jax.numpy as jnp
from jax import lax
from jax.experimental import pallas as pl
from jax.experimental.pallas import tpu as pltpu
from jax.sharding import PartitionSpec as P

HEAD_DIM = 64
STATE = 128
GROUP = 256
EPS = 1e-05
EXTRA = 8
LIMIT = 16 * 1024 * 1024
SEND_ORDER = (0, 1, 2, 3, 4, 5, 6, 7)
BACK_ORDER = (0, 1, 6, 2, 5, 4, 3, 7)
LOG2E = 1.4426950408889634

F32 = jnp.float32
BF16 = jnp.bfloat16
VMEM = pl.BlockSpec(memory_space=pltpu.VMEM)
SMEM = pl.BlockSpec(memory_space=pltpu.SMEM)


def in_hbm(value):
    return pltpu.with_memory_space_constraint(value, pltpu.HBM)


def params(limit=LIMIT):
    return pltpu.CompilerParams(vmem_limit_bytes=limit)


def cost(flops, moved, exps=0):
    return pl.CostEstimate(flops=flops, bytes_accessed=moved, transcendentals=exps)


def turns(order, size):
    last = size - 1
    return [(m, m ^ last if 0 < m < last else m) for m in order if m < size]


def partner(pair):
    even, odd = pair
    return even + (lax.axis_index("head") % 2) * (odd - even)


def position(size):
    return lax.axis_index("seq") % size


def halves(value, count):
    terms = []
    for _ in range(count):
        term = value.astype(BF16)
        terms.append(term)
        value = value - term.astype(F32)
    return jnp.concatenate(terms, axis=1)


def picks(first_head, heads, lanes, width, count):
    row = lax.broadcasted_iota(jnp.int32, (heads, lanes), 0)
    col = lax.broadcasted_iota(jnp.int32, (heads, lanes), 1)
    pick = jnp.where(row == first_head + col // width, 1.0, 0.0).astype(BF16)
    return jnp.concatenate([pick] * count, axis=0)


def project_kernel(tiles, hidden, weight, out, rows_held, weight_held, sems):
    tile = hidden.shape[1] // tiles
    copies = []
    for k in range(tiles):
        row = pl.multiple_of(lax.axis_index("head") * hidden.shape[1] + k * tile, tile)
        pair = (
            pltpu.make_async_copy(
                hidden.at[:, pl.ds(k * tile, tile)], rows_held.at[k], sems.at[0, k]
            ),
            pltpu.make_async_copy(weight.at[pl.ds(row, tile), :], weight_held.at[k], sems.at[1, k]),
        )
        for copy in pair:
            copy.start()
        copies.append(pair)
    total = jnp.zeros(out.shape, F32)
    for k in range(tiles):
        for copy in copies[k]:
            copy.wait()
        total = total + jnp.dot(rows_held[k], weight_held[k], preferred_element_type=F32)
    out[...] = total


def project(hidden, weight):
    rows, depth = hidden.shape
    cols = weight.shape[1]
    tiles = 2
    tile = depth // tiles
    return pl.pallas_call(
        functools.partial(project_kernel, tiles),
        in_specs=[
            pl.BlockSpec(memory_space=pltpu.HBM),
            pl.BlockSpec(memory_space=pltpu.HBM),
        ],
        out_specs=VMEM,
        out_shape=jax.ShapeDtypeStruct((rows, cols), F32),
        scratch_shapes=[
            pltpu.VMEM((tiles, rows, tile), BF16),
            pltpu.VMEM((tiles, tile, cols), BF16),
            pltpu.SemaphoreType.DMA((2, tiles)),
        ],
        compiler_params=params(),
        cost_estimate=cost(2 * rows * depth * cols, 2 * rows * depth + 2 * depth * cols),
        name="project",
    )(in_hbm(hidden), in_hbm(weight))


def decay_kernel(tiles, step_rows, rate, x, weighted, cum, cum_rows, ends, step_out, held, sems):
    heads, rows = step_rows.shape
    cols = x.shape[1]
    lanes = cols // tiles
    copies = []
    for at in range(tiles):
        here = pl.ds(at * lanes, lanes)
        copies.append(pltpu.make_async_copy(x.at[:, here], held.at[at], sems.at[at]))
        copies[-1].start()
    step = step_rows[...].T
    step_out[...] = step
    log_decay = -step * rate[...]
    t = lax.broadcasted_iota(jnp.int32, (rows, rows), 0)
    s = lax.broadcasted_iota(jnp.int32, (rows, rows), 1)
    lower = jnp.where(s <= t, 1.0, 0.0).astype(BF16)
    parts = jnp.dot(lower, halves(log_decay, 3), preferred_element_type=F32)
    total = parts[:, :heads] + (parts[:, heads : 2 * heads] + parts[:, 2 * heads :])
    cum[...] = total
    cum_rows[...] = total.T
    last = total[rows - 1 :, :]
    factor = halves(jnp.exp(last - total) * step, 3)
    final = halves(jnp.broadcast_to(jnp.exp(last), (EXTRA, heads)), 3)
    both = jnp.concatenate([factor, final], axis=0)
    wides = []
    for at in range(tiles):
        here = slice(at * lanes, (at + 1) * lanes)
        pick = picks(at * (lanes // HEAD_DIM), heads, lanes, HEAD_DIM, 3)
        wide = jnp.dot(both, pick, preferred_element_type=F32)
        wides.append(wide[:rows])
        end = wide[rows:]
        high = end.astype(BF16).astype(F32)
        middle = (end - high).astype(BF16).astype(F32)
        low = end - high - middle
        row = lax.broadcasted_iota(jnp.int32, end.shape, 0)
        ends[:, here] = jnp.where(row == 0, high, jnp.where(row == 1, middle, low)).astype(BF16)
    for at in range(tiles):
        copies[at].wait()
        here = slice(at * lanes, (at + 1) * lanes)
        weighted[:, here] = (held[at].astype(F32) * wides[at]).astype(BF16)


def decays(step_rows, rate, x):
    heads, rows = step_rows.shape
    cols = x.shape[1]
    tiles = max(1, cols // 1024)
    return pl.pallas_call(
        functools.partial(decay_kernel, tiles),
        in_specs=[VMEM, VMEM, pl.BlockSpec(memory_space=pltpu.HBM)],
        out_specs=[VMEM] * 6,
        out_shape=[
            jax.ShapeDtypeStruct((rows, cols), BF16),
            jax.ShapeDtypeStruct((rows, heads), F32),
            jax.ShapeDtypeStruct((heads, rows), F32),
            jax.ShapeDtypeStruct((EXTRA, cols), BF16),
            jax.ShapeDtypeStruct((rows, heads), F32),
            jax.ShapeDtypeStruct((tiles, rows, cols // tiles), BF16),
        ],
        scratch_shapes=[pltpu.SemaphoreType.DMA((tiles,))],
        compiler_params=params(),
        cost_estimate=cost(2 * rows * cols * 256, 4 * rows * cols, 2 * rows * heads),
        name="decays",
    )(step_rows, rate, in_hbm(x))


def fresh_kernel(order, n, *refs):
    parts, (weighted, ends, proj), slices = refs[:n], refs[n : n + 3], refs[n + 3 :]
    size = len(slices)
    place = position(size)
    total = parts[0][...]
    for part in parts[1:]:
        total = total + part[...]
    rounded = total.astype(BF16)
    proj[...] = rounded
    width = weighted.shape[1] // size
    b_rows = rounded[:, :STATE]
    for m, pair in enumerate(order):
        cols = pl.ds(pl.multiple_of((place ^ partner(pair)) * width, width), width)
        state = lax.dot_general(
            b_rows, weighted[:, cols], (((0,), (0,)), ((), ())), preferred_element_type=F32
        )
        slices[m][:STATE, :] = state.astype(BF16)
        slices[m][STATE:, :] = ends[:, cols]


def fresh_states(order, parts, weighted, ends):
    rows, cols = weighted.shape
    size = len(order)
    width = cols // size
    n = len(parts)
    return pl.pallas_call(
        functools.partial(fresh_kernel, order, n),
        in_specs=[VMEM] * (n + 2),
        out_specs=[VMEM] * (1 + size),
        out_shape=[jax.ShapeDtypeStruct((rows, 2 * STATE), BF16)]
        + [jax.ShapeDtypeStruct((STATE + EXTRA, width), BF16)] * size,
        compiler_params=params(),
        cost_estimate=cost(2 * rows * cols * STATE, 4 * rows * cols),
        name="fresh",
    )(*parts, weighted, ends)


def gather_factors(order, slices, factors):
    place = position(len(order))
    for pair, piece in zip(order, slices):
        tail = piece[STATE:, :].astype(F32)
        factors[place ^ partner(pair)] = jnp.broadcast_to(tail[0:1] + (tail[1:2] + tail[2:3]), factors.shape[1:])


def total_kernel(order, *refs):
    place = position(len(order))
    slices, (token, out, decay, factors) = refs[:-4], refs[-4:]
    size = len(slices)
    gather_factors(order, slices, factors)
    product = jnp.ones(factors.shape[1:], F32)
    for j in reversed(range(size)):
        factor = factors[j]
        factors[j] = product
        product = product * factor
    decay[...] = product
    scales = [factors[place ^ partner(pair)][:1] for pair in order]
    step = 16
    for row in range(0, STATE, step):
        rows = slice(row, row + step)
        total = jnp.zeros((step, out.shape[1]), F32)
        for scale, piece in zip(scales, slices):
            total = total + scale * piece[rows, :].astype(F32)
        out[rows, :] = total.astype(BF16)


def group_total(order, slices, token):
    size = len(slices)
    width = slices[0].shape[1]
    return pl.pallas_call(
        functools.partial(total_kernel, order),
        in_specs=[VMEM] * (size + 1),
        out_specs=[VMEM] * 2,
        out_shape=[
            jax.ShapeDtypeStruct((STATE, width), BF16),
            jax.ShapeDtypeStruct((8, width), F32),
        ],
        scratch_shapes=[pltpu.VMEM((size, 8, width), F32)],
        compiler_params=params(),
        cost_estimate=cost(2 * size * STATE * width, 2 * size * STATE * width),
        name="total",
    )(*slices, token)


def local_kernel(order, back_order, *refs):
    place = position(len(order))
    slices, (states, scales, ordered, factors) = refs[:-4], refs[-4:]
    size = len(slices)
    gather_factors(order, slices, factors)
    for pair, piece in zip(order, slices):
        ordered[place ^ partner(pair)] = piece[:STATE, :]
    running = jnp.zeros(states.shape[1:], F32)
    product = jnp.ones(factors.shape[1:], F32)
    for j in range(size):
        at = jnp.int32(0)
        for i, pair in enumerate(back_order):
            at = jnp.where(place ^ j == partner(pair), i, at)
        states[at] = running
        scales[at] = product
        running = running * factors[j][:1] + ordered[j].astype(F32)
        product = product * factors[j]


def local_states(order, back_order, slices):
    size = len(slices)
    width = slices[0].shape[1]
    return pl.pallas_call(
        functools.partial(local_kernel, order, back_order),
        in_specs=[VMEM] * size,
        out_specs=[VMEM] * 2,
        out_shape=[
            jax.ShapeDtypeStruct((size, STATE, width), F32),
            jax.ShapeDtypeStruct((size, 8, width), F32),
        ],
        scratch_shapes=[
            pltpu.VMEM((size, STATE, width), BF16),
            pltpu.VMEM((size, 8, width), F32),
        ],
        compiler_params=params(),
        cost_estimate=cost(2 * size * STATE * width, 6 * size * STATE * width),
        name="local",
    )(*slices)


def enter_kernel(states, scales, before, token, *outs):
    group = lax.axis_index("seq") // len(outs)
    entering = jnp.where(group > 0, before[...].astype(F32), 0.0)
    for m, out in enumerate(outs):
        out[...] = (entering * scales[m][:1] + states[m]).astype(BF16)


def entering_states(states, scales, before, token):
    size, _, width = states.shape
    return pl.pallas_call(
        enter_kernel,
        in_specs=[VMEM] * 4,
        out_specs=[VMEM] * size,
        out_shape=[jax.ShapeDtypeStruct((STATE, width), BF16)] * size,
        compiler_params=params(),
        cost_estimate=cost(2 * size * STATE * width, 6 * size * STATE * width),
        name="entering",
    )(states, scales, before, token)


def inner_kernel(size, order, leads, proj, cum, cum_rows, step, x, gate, base, slope, *refs):
    if leads:
        token, held, scores, mixed, sems = refs
    else:
        token, scores, mixed = refs
    rows, heads = cum.shape
    width = base.shape[2]
    here = width // HEAD_DIM
    half = rows // 2
    place = position(size)

    def gate_copy(at):
        cols = pl.ds(pl.multiple_of((place ^ entry(order, at)) * width, width), width)
        return pltpu.make_async_copy(gate.at[:, cols], held.at[at], sems.at[at])

    if leads:
        for at in range(len(order)):
            gate_copy(at).start()
    all_scores = lax.dot_general(
        proj[:, STATE:], proj[:, :STATE], (((1,), (1,)), ((), ())), preferred_element_type=F32
    )
    t = lax.broadcasted_iota(jnp.int32, (half, half), 0)
    s = lax.broadcasted_iota(jnp.int32, (half, half), 1)
    scores[0] = jnp.where(s <= t, all_scores[:half, :half], 0.0)
    scores[1] = jnp.where(s <= t, all_scores[half:, half:], 0.0)
    lower = all_scores[half:, :half].astype(BF16)
    total = cum[...]
    middle = total[half - 1 : half, :]
    grown = jnp.exp(total)
    later = jnp.concatenate(
        [jnp.exp(middle - total[:half]) * step[:half, :], jnp.exp(total[half:] - middle)], axis=0
    )
    per_head = jnp.concatenate([halves(value, 3) for value in (step[...], grown, later)], axis=0)
    parts = halves(total * LOG2E, 3)
    token[...] = jnp.zeros(token.shape, F32)
    lane = lax.broadcasted_iota(jnp.int32, (half, 2 * HEAD_DIM), 1)
    first_head = jnp.where(lane < HEAD_DIM, 1.0, 0.0).astype(BF16)
    second_head = jnp.where(lane < HEAD_DIM, 0.0, 1.0).astype(BF16)

    def one(at, carry):
        owner = place ^ entry(order if leads else order[-base.shape[0] :], at)
        first = owner * here
        wide = jnp.dot(per_head, picks(first, heads, width, HEAD_DIM, 3), preferred_element_type=F32)
        columns = jnp.dot(
            parts, picks(first, heads, here * half, half, 3), preferred_element_type=F32
        )
        each = x.shape[2] // width
        piece = pl.ds(pl.multiple_of(owner % each * width, width), width)
        values = x[owner // each, :, piece].astype(F32)
        scaled = (values * wide[:rows]).astype(BF16)
        early = (values[:half] * wide[2 * rows : 2 * rows + half]).astype(BF16)
        cross = jnp.dot(lower, early, preferred_element_type=F32) * wide[2 * rows + half :]
        for k in range(0, here, 2):
            pair = slice(k * HEAD_DIM, (k + 2) * HEAD_DIM)
            lines = [cum_rows[pl.ds(first + k + n, 1), :] * LOG2E for n in range(2)]
            for i in range(2):
                span = slice(i * half, (i + 1) * half)
                blocks = []
                for n, line in enumerate(lines):
                    gap = columns[span, (k + n) * half : (k + n + 1) * half] - line[:, span]
                    blocks.append((scores[i] * jnp.exp2(jnp.minimum(gap, 0.0))).astype(BF16))
                both = scaled[span, pair]
                mixed[span, pair] = jnp.dot(
                    jnp.concatenate(blocks, axis=1),
                    jnp.concatenate([both * first_head, both * second_head], axis=0),
                    preferred_element_type=F32,
                )
        if leads:
            gate_copy(at).wait()
            g = held[at].astype(F32)
        else:
            g = gate[at + len(order) - base.shape[0]].astype(F32)
        silu = g / (1.0 + jnp.exp(-g))
        base[at, :half, :] = mixed[:half, :] * silu[:half]
        base[at, half:, :] = (mixed[half:, :] + cross) * silu[half:]
        slope[at] = wide[rows : 2 * rows] * silu
        return carry

    lax.fori_loop(0, base.shape[0], one, 0)
    if leads:
        for at in range(base.shape[0], len(order)):
            gate_copy(at).wait()


def entry(order, at):
    value = jnp.int32(0)
    for i, pair in enumerate(order):
        value = jnp.where(at == i, partner(pair), value)
    return value


def inside(order, start, stop, proj, cum, cum_rows, step, x, gate):
    rows, heads = step.shape
    size, n = len(order), stop - start
    first = start == 0
    width = heads // size * HEAD_DIM
    held = [jax.ShapeDtypeStruct((size, rows, width), BF16)] if first else []
    sems = [pltpu.SemaphoreType.DMA((size,))] if first else []
    return pl.pallas_call(
        functools.partial(inner_kernel, size, order if first else order[:stop], first),
        in_specs=[VMEM] * 5 + [pl.BlockSpec(memory_space=pltpu.HBM) if first else VMEM],
        out_specs=[VMEM] * (3 + len(held)),
        out_shape=[jax.ShapeDtypeStruct((n, rows, width), F32)] * 2
        + [jax.ShapeDtypeStruct((8, STATE), F32)]
        + held,
        scratch_shapes=[
            pltpu.VMEM((2, rows // 2, rows // 2), F32),
            pltpu.VMEM((rows, width), F32),
        ]
        + sems,
        compiler_params=params(),
        cost_estimate=cost(8 * rows * rows * n * width, 12 * rows * n * width, rows * rows * heads),
        name="inner",
    )(proj, cum, cum_rows, step, x, in_hbm(gate) if first else gate)


def outer_kernel(prior, first, proj, base, slope, *refs):
    states, (gated, squares) = refs[:-2], refs[-2:]
    c_rows = proj[:, STATE:]
    if prior:
        total, states = states[0][...], states[1:]
    else:
        total = jnp.zeros(squares.shape, F32)
    for m, state in enumerate(states):
        read = jnp.dot(c_rows, state[...], preferred_element_type=F32)
        value = base[first + m] + slope[first + m] * read
        gated[m] = value
        square = value * value
        for k in range(value.shape[1] // STATE):
            total = total + square[:, k * STATE : (k + 1) * STATE]
    squares[...] = total


def outer_part(first, proj, base, slope, prior, states):
    n = len(states)
    _, rows, width = base.shape
    states = [*prior, *states]
    return pl.pallas_call(
        functools.partial(outer_kernel, len(prior), first),
        in_specs=[VMEM] * (len(states) + 3),
        out_specs=[VMEM] * 2,
        out_shape=[
            jax.ShapeDtypeStruct((n, rows, width), F32),
            jax.ShapeDtypeStruct((rows, STATE), F32),
        ],
        compiler_params=params(),
        cost_estimate=cost(2 * rows * n * width * STATE, 12 * rows * n * width),
        name="outer",
    )(proj, base, slope, *states)


def norm_kernel(count, order, n, k, gain, *refs):
    place = position(len(order))
    parts, gated, (out, held, sems) = refs[:n], refs[n : n + k], refs[n + k :]
    total = parts[0][...]
    for part in parts[1:]:
        total = total + part[...]
    mean = jnp.sum(total, axis=1, keepdims=True) * (1.0 / count)
    scale = lax.rsqrt(mean + EPS)
    copies = []
    width = held.shape[2]
    pieces = [(ref, i) for ref in gated for i in range(ref.shape[0])]
    for at, (ref, i) in enumerate(pieces):
        cols = pl.ds(pl.multiple_of((place ^ partner(order[at])) * width, width), width)
        held[at] = (ref[i] * scale * gain[:, cols]).astype(BF16)
        copy = pltpu.make_async_copy(held.at[at], out.at[:, cols], sems.at[at])
        copy.start()
        copies.append(copy)
    for copy in copies:
        copy.wait()


def normalise(count, order, parts, gated, gain):
    size = len(order)
    _, rows, width = gated[0].shape
    cols = size * width
    n, k = len(parts), len(gated)
    return pl.pallas_call(
        functools.partial(norm_kernel, count, order, n, k),
        in_specs=[VMEM] * (1 + n + k),
        out_specs=pl.BlockSpec(memory_space=pltpu.HBM),
        out_shape=jax.ShapeDtypeStruct((rows, cols), BF16),
        scratch_shapes=[pltpu.VMEM((size, rows, width), BF16), pltpu.SemaphoreType.DMA((size,))],
        compiler_params=params(),
        cost_estimate=cost(4 * rows * cols, 6 * rows * cols),
        name="norm",
    )(gain, *parts, *gated)


def swap(value, axis, mask):
    pairs = [(i, i ^ mask) for i in range(lax.axis_size(axis))]
    return lax.ppermute(value, axis, pairs)


def exchange(value, pair):
    count = lax.axis_size("head")
    pairs = [
        (i * count + c, (i ^ pair[c % 2]) * count + c)
        for i in range(lax.axis_size("seq"))
        for c in range(count)
    ]
    return lax.ppermute(value, ("seq", "head"), pairs)


def terms_of_sum(value, axis):
    mask = 1
    terms = [value]
    while mask < lax.axis_size(axis):
        if len(terms) > 1:
            terms = [sum(terms[1:], terms[0])]
        terms.append(swap(terms[0], axis, mask))
        mask *= 2
    return terms


def shards(hidden, weight, head_input, gate_input, step, rate, gain):
    heads = step.shape[1]
    devices = lax.axis_size("seq")
    size = 8
    while devices % size or heads % size or (heads // size * HEAD_DIM) % STATE:
        size //= 2
    groups = devices // size

    order = turns(SEND_ORDER, size)
    back_order = turns(BACK_ORDER, size)

    with jax.named_scope("projection"):
        parts = terms_of_sum(project(hidden, weight), "head")
    with jax.named_scope("decays"):
        weighted, cum, cum_rows, ends, step, x = decays(
            step.T, rate.reshape(1, heads), head_input
        )
    with jax.named_scope("states"):
        proj, *mine = fresh_states(order, parts, weighted, ends)
    with jax.named_scope("to_owners"):
        slices = [mine[0]] + [exchange(part, pair) for pair, part in zip(order[1:], mine[1:])]
    with jax.named_scope("inner"):
        ends_at = sorted({size // 2 + 1, size})
        bounds = list(zip([0] + ends_at[:-1], ends_at))
        inner, gate = [], gate_input
        for a, b in bounds:
            *made, gate = [*inside(back_order, a, b, proj, cum, cum_rows, step, x, gate), gate][:4]
            inner.append(made)
    with jax.named_scope("groups"):
        total, decay = group_total(order, slices, inner[0][2])
        up = [(i, (i + size) % devices) for i in range(devices)]
        before = jnp.zeros_like(total)
        for k in range(groups - 1):
            if k > 0:
                prior = jnp.where(lax.axis_index("seq") // size > 0, before.astype(F32), 0.0)
                sent = (prior * decay[:1] + total.astype(F32)).astype(BF16)
            else:
                sent = total
            before = lax.ppermute(sent, "seq", up)
        states, scales = local_states(order, back_order, slices)
    with jax.named_scope("from_owners"):
        outs = entering_states(states, scales, before, inner[min(1, len(inner) - 1)][2])
        back = [outs[0]] + [exchange(out, pair) for pair, out in zip(back_order[1:], outs[1:])]
    with jax.named_scope("outer"):
        gated, squares = [], []
        for (a, b), (base, slope, _) in zip(bounds, inner):
            cut = b - 1 if b == size and b - a > 1 else b
            for i, j in ((a, cut), (cut, b)):
                if i < j:
                    value, total = outer_part(i - a, proj, base, slope, squares, back[i:j])
                    gated.append(value)
                    squares = [total]
    with jax.named_scope("norm"):
        count = head_input.shape[1] * lax.axis_size("head")
        sums = terms_of_sum(squares[0], "head")
        return normalise(count, back_order, sums, gated, gain.reshape(1, -1))


def solution(mesh):
    in_specs = (
        P("seq", "head"),
        P(),
        P("seq", "head"),
        P("seq", "head"),
        P("seq", "head"),
        P("head"),
        P("head"),
    )
    return jax.shard_map(
        shards, mesh=mesh, in_specs=in_specs, out_specs=P("seq", "head"), check_vma=False
    )
```

```python
import functools

import jax
import jax.numpy as jnp
from jax import lax
from jax.experimental import pallas as pl
from jax.experimental.pallas import tpu as pltpu
from jax.sharding import PartitionSpec as P

HEAD_DIM = 64
STATE = 128
GROUP = 256
EPS = 1e-05
EXTRA = 8
LIMIT = 16 * 1024 * 1024
SEND_ORDER = (0, 1, 2, 3, 4, 5, 6, 7)
BACK_ORDER = (0, 1, 6, 2, 5, 3, 4, 7)
LOG2E = 1.4426950408889634

F32 = jnp.float32
BF16 = jnp.bfloat16
VMEM = pl.BlockSpec(memory_space=pltpu.VMEM)
SMEM = pl.BlockSpec(memory_space=pltpu.SMEM)


def in_hbm(value):
    return pltpu.with_memory_space_constraint(value, pltpu.HBM)


def params(limit=LIMIT):
    return pltpu.CompilerParams(vmem_limit_bytes=limit)


def cost(flops, moved, exps=0):
    return pl.CostEstimate(flops=flops, bytes_accessed=moved, transcendentals=exps)


def message(width):
    groups = width // STATE
    return groups * STATE, groups * STATE + -(-2 * groups // 8) * 8


def turns(order, size):
    last = size - 1
    return [(m, m ^ last if 0 < m < last else m) for m in order if m < size]


def partner(pair):
    even, odd = pair
    return even + (lax.axis_index("head") % 2) * (odd - even)


def position(size):
    return lax.axis_index("seq") % size


def halves(value, count):
    terms = []
    for _ in range(count):
        term = value.astype(BF16)
        terms.append(term)
        value = value - term.astype(F32)
    return jnp.concatenate(terms, axis=1)


def picks(first_head, heads, lanes, width, count):
    row = lax.broadcasted_iota(jnp.int32, (heads, lanes), 0)
    col = lax.broadcasted_iota(jnp.int32, (heads, lanes), 1)
    pick = jnp.where(row == first_head + col // width, 1.0, 0.0).astype(BF16)
    return jnp.concatenate([pick] * count, axis=0)


def project_kernel(tiles, hidden, weight, out, rows_held, weight_held, sems):
    tile = hidden.shape[1] // tiles
    copies = []
    for k in range(tiles):
        row = pl.multiple_of(lax.axis_index("head") * hidden.shape[1] + k * tile, tile)
        pair = (
            pltpu.make_async_copy(
                hidden.at[:, pl.ds(k * tile, tile)], rows_held.at[k], sems.at[0, k]
            ),
            pltpu.make_async_copy(weight.at[pl.ds(row, tile), :], weight_held.at[k], sems.at[1, k]),
        )
        for copy in pair:
            copy.start()
        copies.append(pair)
    total = jnp.zeros(out.shape, F32)
    for k in range(tiles):
        for copy in copies[k]:
            copy.wait()
        total = total + jnp.dot(rows_held[k], weight_held[k], preferred_element_type=F32)
    out[...] = total


def project(hidden, weight):
    rows, depth = hidden.shape
    cols = weight.shape[1]
    tiles = 2
    tile = depth // tiles
    return pl.pallas_call(
        functools.partial(project_kernel, tiles),
        in_specs=[
            pl.BlockSpec(memory_space=pltpu.HBM),
            pl.BlockSpec(memory_space=pltpu.HBM),
        ],
        out_specs=VMEM,
        out_shape=jax.ShapeDtypeStruct((rows, cols), F32),
        scratch_shapes=[
            pltpu.VMEM((tiles, rows, tile), BF16),
            pltpu.VMEM((tiles, tile, cols), BF16),
            pltpu.SemaphoreType.DMA((2, tiles)),
        ],
        compiler_params=params(),
        cost_estimate=cost(2 * rows * depth * cols, 2 * rows * depth + 2 * depth * cols),
        name="project",
    )(in_hbm(hidden), in_hbm(weight))


def decay_kernel(tiles, step_rows, rate, x, weighted, cum, cum_rows, ends, step_out, held, sems):
    heads, rows = step_rows.shape
    cols = x.shape[1]
    lanes = cols // tiles
    copies = []
    for at in range(tiles):
        here = pl.ds(at * lanes, lanes)
        copies.append(pltpu.make_async_copy(x.at[:, here], held.at[at], sems.at[at]))
        copies[-1].start()
    step = step_rows[...].T
    step_out[...] = step
    log_decay = -step * rate[...]
    t = lax.broadcasted_iota(jnp.int32, (rows, rows), 0)
    s = lax.broadcasted_iota(jnp.int32, (rows, rows), 1)
    lower = jnp.where(s <= t, 1.0, 0.0).astype(BF16)
    parts = jnp.dot(lower, halves(log_decay, 3), preferred_element_type=F32)
    total = parts[:, :heads] + (parts[:, heads : 2 * heads] + parts[:, 2 * heads :])
    cum[...] = total
    cum_rows[...] = total.T
    last = total[rows - 1 :, :]
    factor = halves(jnp.exp(last - total) * step, 3)
    final = halves(jnp.broadcast_to(jnp.exp(last), (EXTRA, heads)), 3)
    both = jnp.concatenate([factor, final], axis=0)
    wides = []
    for at in range(tiles):
        here = slice(at * lanes, (at + 1) * lanes)
        pick = picks(at * (lanes // HEAD_DIM), heads, lanes, HEAD_DIM, 3)
        wide = jnp.dot(both, pick, preferred_element_type=F32)
        wides.append(wide[:rows])
        end = wide[rows:]
        high = end.astype(BF16).astype(F32)
        middle = (end - high).astype(BF16).astype(F32)
        low = end - high - middle
        row = lax.broadcasted_iota(jnp.int32, end.shape, 0)
        ends[:, here] = jnp.where(row == 0, high, jnp.where(row == 1, middle, low)).astype(BF16)
    for at in range(tiles):
        copies[at].wait()
        here = slice(at * lanes, (at + 1) * lanes)
        weighted[:, here] = (held[at].astype(F32) * wides[at]).astype(BF16)


def decays(step_rows, rate, x):
    heads, rows = step_rows.shape
    cols = x.shape[1]
    tiles = max(1, cols // 1024)
    return pl.pallas_call(
        functools.partial(decay_kernel, tiles),
        in_specs=[VMEM, VMEM, pl.BlockSpec(memory_space=pltpu.HBM)],
        out_specs=[VMEM] * 6,
        out_shape=[
            jax.ShapeDtypeStruct((rows, cols), BF16),
            jax.ShapeDtypeStruct((rows, heads), F32),
            jax.ShapeDtypeStruct((heads, rows), F32),
            jax.ShapeDtypeStruct((EXTRA, cols), BF16),
            jax.ShapeDtypeStruct((rows, heads), F32),
            jax.ShapeDtypeStruct((tiles, rows, cols // tiles), BF16),
        ],
        scratch_shapes=[pltpu.SemaphoreType.DMA((tiles,))],
        compiler_params=params(),
        cost_estimate=cost(2 * rows * cols * 256, 4 * rows * cols, 2 * rows * heads),
        name="decays",
    )(step_rows, rate, in_hbm(x))


def fresh_kernel(order, n, *refs):
    parts, (weighted, ends, proj), slices = refs[:n], refs[n : n + 3], refs[n + 3 :]
    size = len(slices)
    place = position(size)
    total = parts[0][...]
    for part in parts[1:]:
        total = total + part[...]
    rounded = total.astype(BF16)
    proj[...] = rounded
    width = weighted.shape[1] // size
    b_rows = rounded[:, :STATE]
    for m, pair in enumerate(order):
        cols = pl.ds(pl.multiple_of((place ^ partner(pair)) * width, width), width)
        state = lax.dot_general(
            b_rows, weighted[:, cols], (((0,), (0,)), ((), ())), preferred_element_type=F32
        )
        end = ends[:, cols].astype(F32)
        body, whole = message(width)
        tail = []
        for g in range(width // STATE):
            lanes = slice(g * STATE, (g + 1) * STATE)
            slices[m][lanes, :] = state[:, lanes].astype(BF16)
            tail.append(end[:2, lanes])
        tail.append(jnp.zeros((whole - body - 2 * len(tail), STATE), F32))
        tail = [part for part in tail if part.shape[0]]
        slices[m][body:, :] = jnp.concatenate(tail, axis=0).astype(BF16)


def fresh_states(order, parts, weighted, ends):
    rows, cols = weighted.shape
    size = len(order)
    width = cols // size
    n = len(parts)
    return pl.pallas_call(
        functools.partial(fresh_kernel, order, n),
        in_specs=[VMEM] * (n + 2),
        out_specs=[VMEM] * (1 + size),
        out_shape=[jax.ShapeDtypeStruct((rows, 2 * STATE), BF16)]
        + [jax.ShapeDtypeStruct((message(width)[1], STATE), BF16)] * size,
        compiler_params=params(),
        cost_estimate=cost(2 * rows * cols * STATE, 4 * rows * cols),
        name="fresh",
    )(*parts, weighted, ends)


def gather_factors(order, slices, factors):
    place = position(len(order))
    for pair, piece in zip(order, slices):
        width = factors.shape[2]
        tail = piece[message(width)[0] :, :].astype(F32)
        terms = [tail[2 * g : 2 * g + 1] + tail[2 * g + 1 : 2 * g + 2] for g in range(width // STATE)]
        factors[place ^ partner(pair)] = jnp.broadcast_to(
            jnp.concatenate(terms, axis=1), factors.shape[1:]
        )


def total_kernel(order, *refs):
    place = position(len(order))
    slices, (token, out, decay, factors) = refs[:-4], refs[-4:]
    size = len(slices)
    gather_factors(order, slices, factors)
    product = jnp.ones(factors.shape[1:], F32)
    for j in reversed(range(size)):
        factor = factors[j]
        factors[j] = product
        product = product * factor
    decay[...] = product
    scales = [factors[place ^ partner(pair)][:1] for pair in order]
    step = 64
    for g in range(out.shape[1] // STATE):
        lanes = slice(g * STATE, (g + 1) * STATE)
        for row in range(0, STATE, step):
            total = jnp.zeros((step, STATE), F32)
            for scale, piece in zip(scales, slices):
                rows = slice(g * STATE + row, g * STATE + row + step)
                total = total + scale[:, lanes] * piece[rows, :].astype(F32)
            out[row : row + step, lanes] = total.astype(BF16)


def lanes_of(piece):
    return piece.shape[0] // STATE * STATE


def group_total(order, slices, token):
    size = len(slices)
    width = lanes_of(slices[0])
    return pl.pallas_call(
        functools.partial(total_kernel, order),
        in_specs=[VMEM] * (size + 1),
        out_specs=[VMEM] * 2,
        out_shape=[
            jax.ShapeDtypeStruct((STATE, width), BF16),
            jax.ShapeDtypeStruct((8, width), F32),
        ],
        scratch_shapes=[pltpu.VMEM((size, 8, width), F32)],
        compiler_params=params(),
        cost_estimate=cost(2 * size * STATE * width, 2 * size * STATE * width),
        name="total",
    )(*slices, token)


def local_kernel(order, back_order, *refs):
    place = position(len(order))
    slices, (states, scales, ordered, factors) = refs[:-4], refs[-4:]
    size = len(slices)
    gather_factors(order, slices, factors)
    for pair, piece in zip(order, slices):
        ordered[place ^ partner(pair)] = piece[: ordered.shape[1], :]
    running = jnp.zeros(states.shape[1:], F32)
    product = jnp.ones(factors.shape[1:], F32)
    for j in range(size):
        at = jnp.int32(0)
        for i, pair in enumerate(back_order):
            at = jnp.where(place ^ j == partner(pair), i, at)
        states[at] = running
        scales[at] = product
        fresh = [
            ordered[j, g * STATE : (g + 1) * STATE, :].astype(F32)
            for g in range(running.shape[1] // STATE)
        ]
        running = running * factors[j][:1] + jnp.concatenate(fresh, axis=1)
        product = product * factors[j]


def local_states(order, back_order, slices):
    size = len(slices)
    width = lanes_of(slices[0])
    return pl.pallas_call(
        functools.partial(local_kernel, order, back_order),
        in_specs=[VMEM] * size,
        out_specs=[VMEM] * 2,
        out_shape=[
            jax.ShapeDtypeStruct((size, STATE, width), F32),
            jax.ShapeDtypeStruct((size, 8, width), F32),
        ],
        scratch_shapes=[
            pltpu.VMEM((size, width, STATE), BF16),
            pltpu.VMEM((size, 8, width), F32),
        ],
        compiler_params=params(),
        cost_estimate=cost(2 * size * STATE * width, 6 * size * STATE * width),
        name="local",
    )(*slices)


def enter_kernel(states, scales, before, token, *outs):
    group = lax.axis_index("seq") // len(outs)
    entering = jnp.where(group > 0, before[...].astype(F32), 0.0)
    for m, out in enumerate(outs):
        out[...] = (entering * scales[m][:1] + states[m]).astype(BF16)


def entering_states(states, scales, before, token):
    size, _, width = states.shape
    return pl.pallas_call(
        enter_kernel,
        in_specs=[VMEM] * 4,
        out_specs=[VMEM] * size,
        out_shape=[jax.ShapeDtypeStruct((STATE, width), BF16)] * size,
        compiler_params=params(),
        cost_estimate=cost(2 * size * STATE * width, 6 * size * STATE * width),
        name="entering",
    )(states, scales, before, token)


def inner_kernel(size, order, leads, proj, cum, cum_rows, step, x, gate, base, slope, *refs):
    if leads:
        token, held, scores, mixed, sems = refs
    else:
        token, scores, mixed = refs
    rows, heads = cum.shape
    width = base.shape[2]
    here = width // HEAD_DIM
    half = rows // 2
    place = position(size)

    def gate_copy(at):
        cols = pl.ds(pl.multiple_of((place ^ entry(order, at)) * width, width), width)
        return pltpu.make_async_copy(gate.at[:, cols], held.at[at], sems.at[at])

    if leads:
        for at in range(len(order)):
            gate_copy(at).start()
    all_scores = lax.dot_general(
        proj[:, STATE:], proj[:, :STATE], (((1,), (1,)), ((), ())), preferred_element_type=F32
    )
    t = lax.broadcasted_iota(jnp.int32, (half, half), 0)
    s = lax.broadcasted_iota(jnp.int32, (half, half), 1)
    scores[0] = jnp.where(s <= t, all_scores[:half, :half], 0.0)
    scores[1] = jnp.where(s <= t, all_scores[half:, half:], 0.0)
    lower = all_scores[half:, :half].astype(BF16)
    total = cum[...]
    middle = total[half - 1 : half, :]
    grown = jnp.exp(total)
    later = jnp.concatenate(
        [jnp.exp(middle - total[:half]) * step[:half, :], jnp.exp(total[half:] - middle)], axis=0
    )
    per_head = jnp.concatenate([halves(value, 3) for value in (step[...], grown, later)], axis=0)
    parts = halves(total * LOG2E, 3)
    token[...] = jnp.zeros(token.shape, F32)
    lane = lax.broadcasted_iota(jnp.int32, (half, 2 * HEAD_DIM), 1)
    first_head = jnp.where(lane < HEAD_DIM, 1.0, 0.0).astype(BF16)
    second_head = jnp.where(lane < HEAD_DIM, 0.0, 1.0).astype(BF16)

    def one(at, carry):
        owner = place ^ entry(order if leads else order[-base.shape[0] :], at)
        first = owner * here
        wide = jnp.dot(per_head, picks(first, heads, width, HEAD_DIM, 3), preferred_element_type=F32)
        columns = jnp.dot(
            parts, picks(first, heads, here * half, half, 3), preferred_element_type=F32
        )
        each = x.shape[2] // width
        piece = pl.ds(pl.multiple_of(owner % each * width, width), width)
        values = x[owner // each, :, piece].astype(F32)
        scaled = (values * wide[:rows]).astype(BF16)
        early = (values[:half] * wide[2 * rows : 2 * rows + half]).astype(BF16)
        cross = jnp.dot(lower, early, preferred_element_type=F32) * wide[2 * rows + half :]
        for k in range(0, here, 2):
            pair = slice(k * HEAD_DIM, (k + 2) * HEAD_DIM)
            lines = [cum_rows[pl.ds(first + k + n, 1), :] * LOG2E for n in range(2)]
            for i in range(2):
                span = slice(i * half, (i + 1) * half)
                blocks = []
                for n, line in enumerate(lines):
                    gap = columns[span, (k + n) * half : (k + n + 1) * half] - line[:, span]
                    blocks.append((scores[i] * jnp.exp2(jnp.minimum(gap, 0.0))).astype(BF16))
                both = scaled[span, pair]
                mixed[span, pair] = jnp.dot(
                    jnp.concatenate(blocks, axis=1),
                    jnp.concatenate([both * first_head, both * second_head], axis=0),
                    preferred_element_type=F32,
                )
        if leads:
            gate_copy(at).wait()
            g = held[at].astype(F32)
        else:
            g = gate[at + len(order) - base.shape[0]].astype(F32)
        silu = g / (1.0 + jnp.exp(-g))
        base[at, :half, :] = mixed[:half, :] * silu[:half]
        base[at, half:, :] = (mixed[half:, :] + cross) * silu[half:]
        slope[at] = wide[rows : 2 * rows] * silu
        return carry

    lax.fori_loop(0, base.shape[0], one, 0)
    if leads:
        for at in range(base.shape[0], len(order)):
            gate_copy(at).wait()


def entry(order, at):
    value = jnp.int32(0)
    for i, pair in enumerate(order):
        value = jnp.where(at == i, partner(pair), value)
    return value


def inside(order, start, stop, proj, cum, cum_rows, step, x, gate):
    rows, heads = step.shape
    size, n = len(order), stop - start
    first = start == 0
    width = heads // size * HEAD_DIM
    held = [jax.ShapeDtypeStruct((size, rows, width), BF16)] if first else []
    sems = [pltpu.SemaphoreType.DMA((size,))] if first else []
    return pl.pallas_call(
        functools.partial(inner_kernel, size, order if first else order[:stop], first),
        in_specs=[VMEM] * 5 + [pl.BlockSpec(memory_space=pltpu.HBM) if first else VMEM],
        out_specs=[VMEM] * (3 + len(held)),
        out_shape=[jax.ShapeDtypeStruct((n, rows, width), F32)] * 2
        + [jax.ShapeDtypeStruct((8, STATE), F32)]
        + held,
        scratch_shapes=[
            pltpu.VMEM((2, rows // 2, rows // 2), F32),
            pltpu.VMEM((rows, width), F32),
        ]
        + sems,
        compiler_params=params(),
        cost_estimate=cost(8 * rows * rows * n * width, 12 * rows * n * width, rows * rows * heads),
        name="inner",
    )(proj, cum, cum_rows, step, x, in_hbm(gate) if first else gate)


def outer_kernel(prior, first, proj, base, slope, *refs):
    states, (gated, squares) = refs[:-2], refs[-2:]
    c_rows = proj[:, STATE:]
    if prior:
        total, states = states[0][...], states[1:]
    else:
        total = jnp.zeros(squares.shape, F32)
    for m, state in enumerate(states):
        read = jnp.dot(c_rows, state[...], preferred_element_type=F32)
        value = base[first + m] + slope[first + m] * read
        gated[m] = value
        square = value * value
        for k in range(value.shape[1] // STATE):
            total = total + square[:, k * STATE : (k + 1) * STATE]
    squares[...] = total


def outer_part(first, proj, base, slope, prior, states):
    n = len(states)
    _, rows, width = base.shape
    states = [*prior, *states]
    return pl.pallas_call(
        functools.partial(outer_kernel, len(prior), first),
        in_specs=[VMEM] * (len(states) + 3),
        out_specs=[VMEM] * 2,
        out_shape=[
            jax.ShapeDtypeStruct((n, rows, width), F32),
            jax.ShapeDtypeStruct((rows, STATE), F32),
        ],
        compiler_params=params(),
        cost_estimate=cost(2 * rows * n * width * STATE, 12 * rows * n * width),
        name="outer",
    )(proj, base, slope, *states)


def norm_kernel(count, order, n, k, gain, *refs):
    place = position(len(order))
    parts, gated, (out, held, sems) = refs[:n], refs[n : n + k], refs[n + k :]
    total = parts[0][...]
    for part in parts[1:]:
        total = total + part[...]
    mean = jnp.sum(total, axis=1, keepdims=True) * (1.0 / count)
    scale = lax.rsqrt(mean + EPS)
    copies = []
    width = held.shape[2]
    pieces = [(ref, i) for ref in gated for i in range(ref.shape[0])]
    for at, (ref, i) in enumerate(pieces):
        cols = pl.ds(pl.multiple_of((place ^ partner(order[at])) * width, width), width)
        held[at] = (ref[i] * scale * gain[:, cols]).astype(BF16)
        copy = pltpu.make_async_copy(held.at[at], out.at[:, cols], sems.at[at])
        copy.start()
        copies.append(copy)
    for copy in copies:
        copy.wait()


def normalise(count, order, parts, gated, gain):
    size = len(order)
    _, rows, width = gated[0].shape
    cols = size * width
    n, k = len(parts), len(gated)
    return pl.pallas_call(
        functools.partial(norm_kernel, count, order, n, k),
        in_specs=[VMEM] * (1 + n + k),
        out_specs=pl.BlockSpec(memory_space=pltpu.HBM),
        out_shape=jax.ShapeDtypeStruct((rows, cols), BF16),
        scratch_shapes=[pltpu.VMEM((size, rows, width), BF16), pltpu.SemaphoreType.DMA((size,))],
        compiler_params=params(),
        cost_estimate=cost(4 * rows * cols, 6 * rows * cols),
        name="norm",
    )(gain, *parts, *gated)


def swap(value, axis, mask):
    pairs = [(i, i ^ mask) for i in range(lax.axis_size(axis))]
    return lax.ppermute(value, axis, pairs)


def exchange(value, pair):
    count = lax.axis_size("head")
    pairs = [
        (i * count + c, (i ^ pair[c % 2]) * count + c)
        for i in range(lax.axis_size("seq"))
        for c in range(count)
    ]
    return lax.ppermute(value, ("seq", "head"), pairs)


def terms_of_sum(value, axis):
    mask = 1
    terms = [value]
    while mask < lax.axis_size(axis):
        if len(terms) > 1:
            terms = [sum(terms[1:], terms[0])]
        terms.append(swap(terms[0], axis, mask))
        mask *= 2
    return terms


def shards(hidden, weight, head_input, gate_input, step, rate, gain):
    heads = step.shape[1]
    devices = lax.axis_size("seq")
    size = 8
    while devices % size or heads % size or (heads // size * HEAD_DIM) % STATE:
        size //= 2
    groups = devices // size

    order = turns(SEND_ORDER, size)
    back_order = turns(BACK_ORDER, size)

    with jax.named_scope("projection"):
        parts = terms_of_sum(project(hidden, weight), "head")
    with jax.named_scope("decays"):
        weighted, cum, cum_rows, ends, step, x = decays(
            step.T, rate.reshape(1, heads), head_input
        )
    with jax.named_scope("states"):
        proj, *mine = fresh_states(order, parts, weighted, ends)
    with jax.named_scope("to_owners"):
        slices = [mine[0]] + [exchange(part, pair) for pair, part in zip(order[1:], mine[1:])]
    with jax.named_scope("inner"):
        ends_at = sorted({size // 2 + 1, size})
        bounds = list(zip([0] + ends_at[:-1], ends_at))
        inner, gate = [], gate_input
        for a, b in bounds:
            *made, gate = [*inside(back_order, a, b, proj, cum, cum_rows, step, x, gate), gate][:4]
            inner.append(made)
    with jax.named_scope("groups"):
        total, decay = group_total(order, slices, inner[0][2])
        up = [(i, (i + size) % devices) for i in range(devices)]
        before = jnp.zeros_like(total)
        for k in range(groups - 1):
            if k > 0:
                prior = jnp.where(lax.axis_index("seq") // size > 0, before.astype(F32), 0.0)
                sent = (prior * decay[:1] + total.astype(F32)).astype(BF16)
            else:
                sent = total
            before = lax.ppermute(sent, "seq", up)
        states, scales = local_states(order, back_order, slices)
    with jax.named_scope("from_owners"):
        outs = entering_states(states, scales, before, inner[min(1, len(inner) - 1)][2])
        back = [outs[0]] + [exchange(out, pair) for pair, out in zip(back_order[1:], outs[1:])]
    with jax.named_scope("outer"):
        gated, squares = [], []
        for (a, b), (base, slope, _) in zip(bounds, inner):
            cut = b - 1 if b == size and b - a > 1 else b
            for i, j in ((a, cut), (cut, b)):
                if i < j:
                    value, total = outer_part(i - a, proj, base, slope, squares, back[i:j])
                    gated.append(value)
                    squares = [total]
    with jax.named_scope("norm"):
        count = head_input.shape[1] * lax.axis_size("head")
        sums = terms_of_sum(squares[0], "head")
        return normalise(count, back_order, sums, gated, gain.reshape(1, -1))


def solution(mesh):
    in_specs = (
        P("seq", "head"),
        P(),
        P("seq", "head"),
        P("seq", "head"),
        P("seq", "head"),
        P("head"),
        P("head"),
    )
    return jax.shard_map(
        shards, mesh=mesh, in_specs=in_specs, out_specs=P("seq", "head"), check_vma=False
    )
```
